32 devices in a mesh: dp: 16 (over z, x, core), fsdp: 2 (over y).
Axes of the slice: x: 2, y: 2, z: 4, core: 2. Of those that a mesh axis runs over, the one named last changes fastest.
Arguments:
- tokens: bfloat16 [4096, 768], P(('dp', 'fsdp')), may hold values from -6 to 6
- query_weight: bfloat16 [768, 768], P(('dp', 'fsdp')), may hold values from -0.21875 to 0.21875
- key_weight: bfloat16 [768, 768], P(('dp', 'fsdp')), may hold values from -0.21875 to 0.21875
- value_weight: bfloat16 [768, 768], P(('dp', 'fsdp')), may hold values from -0.21875 to 0.21875
- query_bias: bfloat16 [768], P(('dp', 'fsdp')), may hold values from -3 to 3
- value_bias: bfloat16 [768], P(('dp', 'fsdp')), may hold values from -3 to 3
- out_weight: bfloat16 [768, 768], P(('dp', 'fsdp')), may hold values from -1.75 to 1.75
- out_bias: bfloat16 [768], P(('dp', 'fsdp')), may hold values from -3 to 3
- first_gain: bfloat16 [768], P(('dp', 'fsdp')), may hold values from 0.25 to 1.75
- first_shift: bfloat16 [768], P(('dp', 'fsdp')), may hold values from -3 to 3
- up_weight: bfloat16 [768, 3072], P(('dp', 'fsdp')), may hold values from -0.21875 to 0.21875
- up_bias: bfloat16 [3072], P(('dp', 'fsdp')), may hold values from -3 to 3
- down_weight: bfloat16 [3072, 768], P(('dp', 'fsdp')), may hold values from -0.109375 to 0.109375
- down_bias: bfloat16 [768], P(('dp', 'fsdp')), may hold values from -3 to 3
- second_gain: bfloat16 [768], P(('dp', 'fsdp')), may hold values from 0.25 to 1.75
- second_shift: bfloat16 [768], P(('dp', 'fsdp')), may hold values from -3 to 3
- segment_ids: int32 [32, 128], P(('dp', 'fsdp')), may hold values from 0 to 2, never falling along the last dimension, each value on 1 to 96 neighbouring positions
- out_grad: bfloat16 [4096, 768], P(('dp', 'fsdp')), may hold values from -12 to 12
Outputs:
- layer_output: bfloat16 [4096, 768], P(('dp', 'fsdp'))
- input_grad: float32 [4096, 768], P(('dp', 'fsdp'))
- grad_query_weight: float32 [768, 768], P(('dp', 'fsdp'))
- grad_key_weight: float32 [768, 768], P(('dp', 'fsdp'))
- grad_value_weight: float32 [768, 768], P(('dp', 'fsdp'))
- grad_query_bias: float32 [768], P(('dp', 'fsdp'))
- grad_value_bias: float32 [768], P(('dp', 'fsdp'))
- grad_out_weight: float32 [768, 768], P(('dp', 'fsdp'))
- grad_out_bias: float32 [768], P(('dp', 'fsdp'))
- grad_first_gain: float32 [768], P(('dp', 'fsdp'))
- grad_first_shift: float32 [768], P(('dp', 'fsdp'))
- grad_up_weight: float32 [768, 3072], P(('dp', 'fsdp'))
- grad_up_bias: float32 [3072], P(('dp', 'fsdp'))
- grad_down_weight: float32 [3072, 768], P(('dp', 'fsdp'))
- grad_down_bias: float32 [768], P(('dp', 'fsdp'))
- grad_second_gain: float32 [768], P(('dp', 'fsdp'))
- grad_second_shift: float32 [768], P(('dp', 'fsdp'))
The draws below stay inside these ranges and needn't reach their ends.
Inputs may be any that keep to these rules, and one draw needn't show every extreme that they name: `segment_ids`: numbers never fall along a sequence; each document holds at most 96 tokens.
All inputs are finite; a program needn't handle non-finite values.
Results may differ from the reference program's by a relative error of at most 0.015.
Values may be sent and summed in bfloat16 or wider, within the bound.
A program may use at most 128 MiB of HBM per device.

```python
import math
import jax
import jax.numpy as jnp
import numpy as np
from jax import lax

D = 768
H = 12
HD = 64
FF = 3072
TOK_DEV = 128
SEQS = 32
TOKENS = 4096


def strengthened(values, key, source, target, shards_of, factor):
    owner, partner = [(jnp.arange(values.shape[axis_at]) // (values.shape[axis_at] // shards_of)).reshape([-1 if axis == axis_at else 1 for axis in range(values.ndim)]) for axis_at in (source, target)]
    chosen = jax.random.permutation(key, shards_of)[partner]
    strong = (owner == chosen) | (owner == (partner + shards_of // 2) % shards_of)
    return jnp.where(strong, factor * values, values)


def shard_levels(stream_key, extent, split, low, top_value):
    level, own = 1.0, jax.random.fold_in(stream_key, 6)
    for axis_at, shards_of in split:
        steps = jnp.exp(jax.random.uniform(jax.random.fold_in(own, axis_at), (shards_of,), jnp.float32, low / len(split), top_value / len(split)))
        level = level * jnp.repeat(steps, extent[axis_at] // shards_of).reshape([-1 if axis == axis_at else 1 for axis in range(len(extent))])
    return level


def length_profile(amount, total, bound, slope):
    portions = [(1 << 20) // math.isqrt(rank ** slope) + 1 for rank in range(2, amount + 1)]
    spare, given = total - bound - (amount - 1), [1] * (amount - 1)
    while spare > 0:
        candidates = [i for i in range(amount - 1) if given[i] < bound]
        whole, budget = sum([portions[i] for i in candidates]), spare
        for i in candidates:
            extra = min(bound - given[i], max(1, budget * portions[i] // whole), spare)
            given[i] = given[i] + extra
            spare = spare - extra
    return np.array([bound] + given)


def uneven(stream_key, number_of, total, reach, lean):
    if number_of == 2:
        one = jax.random.randint(stream_key, (), max(1, total - reach), min(reach, total - 1) + 1)
        return jnp.stack([one, total - one])
    lengths = jnp.asarray(length_profile(number_of, total, reach, lean), jnp.int32)
    twos = (number_of - 1) // 2
    giver, sink = lengths[1:1 + 2 * twos:2], lengths[2:2 + 2 * twos:2]
    margin = jnp.minimum(giver - 1, reach - sink)
    passed = jax.random.randint(jax.random.fold_in(stream_key, 1), (twos,), 0, 1 << 20) % (margin + 1)
    lengths = lengths.at[1:1 + 2 * twos:2].set(giver - passed).at[2:2 + 2 * twos:2].set(sink + passed)
    return lengths[jax.random.permutation(jax.random.fold_in(stream_key, 2), number_of)]


def gaussian(own_key, shape, scale, limit, cuts=(), dtype=jnp.bfloat16):
    drawn = jax.random.normal(own_key, shape, jnp.float32) * scale
    if len(cuts) > 0:
        drawn = shard_levels(own_key, shape, cuts, -0.22, 0.18) * drawn
    return jnp.clip(drawn, min=-limit, max=limit).astype(dtype)


def heavy_noise(own_key, dims, scale, limit, shards, heavy, kind=jnp.bfloat16):
    array = scale * jax.random.normal(own_key, dims, jnp.float32)
    if shards:
        array = array * shard_levels(own_key, dims, shards, -0.22, 0.18)
    return jnp.clip(strengthened(array, jax.random.fold_in(own_key, 3), *heavy), -limit, limit).astype(kind)


def setup_inputs(seed: int = 0) -> dict:
    splits = jax.random.split(jax.random.key(seed), 19)
    return {
        "tokens": gaussian(splits[0], (TOKENS, D), 1.0, 6.0, ((0, 32),)),
        "query_weight": gaussian(splits[1], (D, D), D ** -0.5, 0.21875, ((0, 32),)),
        "key_weight": gaussian(splits[2], (D, D), D ** -0.5, 0.21875, ((0, 32),)),
        "value_weight": gaussian(splits[3], (D, D), D ** -0.5, 0.21875, ((0, 32),)),
        "query_bias": gaussian(splits[4], (D,), 0.5, 3.0, ((0, 32),)),
        "value_bias": gaussian(splits[5], (D,), 0.5, 3.0, ((0, 32),)),
        "out_weight": gaussian(splits[6], (D, D), (D // 64) ** -0.5, 1.75, ((0, 32),)),
        "out_bias": gaussian(splits[7], (D,), 0.5, 3.0, ((0, 32),)),
        "first_gain": jnp.clip(1.0 + 0.15 * jax.random.normal(splits[8], (D,), jnp.float32), 0.25, 1.75).astype(jnp.bfloat16),
        "first_shift": gaussian(splits[9], (D,), 0.5, 3.0, ((0, 32),)),
        "up_weight": gaussian(splits[10], (D, FF), D ** -0.5, 0.21875, ((0, 32),)),
        "up_bias": gaussian(splits[11], (FF,), 0.5, 3.0, ((0, 32),)),
        "down_weight": gaussian(splits[12], (FF, D), FF ** -0.5, 0.109375, ((0, 32),)),
        "down_bias": gaussian(splits[13], (D,), 0.5, 3.0, ((0, 32),)),
        "second_gain": jnp.clip(1.0 + 0.15 * jax.random.normal(splits[14], (D,), jnp.float32), 0.25, 1.75).astype(jnp.bfloat16),
        "second_shift": gaussian(splits[15], (D,), 0.5, 3.0, ((0, 32),)),
        "segment_ids": jax.vmap(lambda own: jnp.searchsorted(jnp.cumsum(uneven(own, 2 + TOK_DEV // 128, TOK_DEV, min(200, TOK_DEV - TOK_DEV // 4), 0)), jnp.arange(TOK_DEV), side="right"))(jax.random.split(splits[16], SEQS)).reshape((SEQS, TOK_DEV)).astype(jnp.int32),
        "out_grad": heavy_noise(splits[17], (TOKENS, D), 1.0, 12.0, ((0, 32),), (0, 1, 32, 2.75)),
    }


HIGH = lax.Precision.HIGHEST
PARAM_NAMES = ['query_weight', 'key_weight', 'value_weight', 'query_bias', 'value_bias', 'out_weight', 'out_bias', 'first_gain', 'first_shift', 'up_weight', 'up_bias', 'down_weight', 'down_bias', 'second_gain', 'second_shift']

@jax.custom_vjp
def low(v):
    return lax.optimization_barrier(v.astype(jnp.bfloat16)).astype(jnp.float32)

@jax.custom_vjp
def low_back(v):
    return v

def low_keep(v):
    return (low(v), None)

def low_pass(kept, grad):
    return (grad,)

def back_keep(v):
    return (v, None)

def back_low(kept, grad):
    return (low(grad),)
low.defvjp(low_keep, low_pass)
low_back.defvjp(back_keep, back_low)

def mult(left, right):
    return jnp.dot(left, right, precision=HIGH)

def layer_norm(rows, gain, shift):
    centred = rows - lax.optimization_barrier(jnp.mean(rows, axis=-1, keepdims=True))
    scale = lax.rsqrt(lax.optimization_barrier(jnp.mean(centred * centred, axis=-1, keepdims=True)) + 1e-06)
    return centred * scale * gain + shift

def attend(query, keys, values, segs):
    length = query.shape[0]
    q_heads = query.reshape(length, H, HD)
    k_heads = keys.reshape(length, H, HD)
    v_heads = values.reshape(length, H, HD)
    scores = low_back(jnp.einsum('qhd,khd->hqk', q_heads, k_heads, precision=HIGH) * 0.125)
    same = segs[:, None] == segs[None, :]
    masked = jnp.where(same[None], scores, -1e+30)
    top = lax.optimization_barrier(jnp.max(masked, axis=-1, keepdims=True))
    expo = jnp.exp(masked - top)
    probs = expo / lax.optimization_barrier(jnp.sum(expo, axis=-1, keepdims=True))
    mixed = jnp.einsum('hqk,khd->qhd', low(probs), v_heads, precision=HIGH)
    return mixed.reshape(length, H * HD)

def layer(rows, segs, weights):
    count = rows.shape[0]
    flat = rows.reshape(-1, D)
    query = low_back(low(mult(flat, weights['query_weight']) + weights['query_bias']))
    keys = low_back(low(mult(flat, weights['key_weight'])))
    values = low_back(low(mult(flat, weights['value_weight']) + weights['value_bias']))
    attended = jax.vmap(attend)(query.reshape(count, -1, D), keys.reshape(count, -1, D), values.reshape(count, -1, D), segs)
    attended = low_back(low(attended.reshape(-1, D)))
    branch = low_back(mult(attended, weights['out_weight']) + weights['out_bias'])
    first = layer_norm(flat + branch, weights['first_gain'], weights['first_shift'])
    hidden = low_back(mult(low(first), weights['up_weight']) + weights['up_bias'])
    active = low(jax.nn.gelu(hidden, approximate=False))
    down = low_back(mult(active, weights['down_weight']) + weights['down_bias'])
    second = layer_norm(first + down, weights['second_gain'], weights['second_shift'])
    return second.reshape(rows.shape)

def reference(tokens, query_weight, key_weight, value_weight, query_bias, value_bias, out_weight, out_bias, first_gain, first_shift, up_weight, up_bias, down_weight, down_bias, second_gain, second_shift, segment_ids, out_grad):
    values_in = [query_weight, key_weight, value_weight, query_bias, value_bias, out_weight, out_bias, first_gain, first_shift, up_weight, up_bias, down_weight, down_bias, second_gain, second_shift]
    weights = {}
    for name, value in zip(PARAM_NAMES, values_in):
        weights[name] = value.astype(jnp.float32)
    group = math.gcd(SEQS, max(1, 4096 // TOK_DEV))
    rounds = SEQS // group
    rows = tokens.astype(jnp.float32).reshape(rounds, group, TOK_DEV, D)
    segs = segment_ids.reshape(rounds, group, TOK_DEV)
    cotangent = out_grad.astype(jnp.float32).reshape(rounds, group, TOK_DEV, D)

    def one_round(total, pieces):
        block, seg_block, grad_block = pieces

        def local_layer(rows_in, weights_in):
            return layer(rows_in, seg_block, weights_in)
        result, backward = jax.vjp(local_layer, block, weights)
        d_rows, d_weights = backward(grad_block)
        total = jax.tree.map(jnp.add, total, d_weights)
        return (total, (result, d_rows))
    zeros = jax.tree.map(jnp.zeros_like, weights)
    total, (results, d_rows) = lax.scan(one_round, zeros, (rows, segs, cotangent))
    outputs = [results.reshape(TOKENS, D).astype(jnp.bfloat16), d_rows.reshape(TOKENS, D)]
    for name in PARAM_NAMES:
        outputs.append(total[name])
    return tuple(outputs)
```

```python
from functools import partial

import jax
import jax.numpy as jnp
from jax import lax
from jax.experimental import pallas as pl
from jax.experimental.pallas import tpu as pltpu
from jax.sharding import PartitionSpec as P

HD = 64
MESH = pl.DeviceIdType.MESH
TILE = 16


def dims_of(dp, fsdp):
    core = (fsdp, 2 if dp % 2 == 0 else 1)
    rest, stride = dp // core[1], fsdp * core[1]
    sizes = []
    while rest > 1:
        step = 2 if rest % 4 else 4
        if not sizes and rest % 2 == 0:
            step = 2
        if rest % step:
            step = rest
        sizes.append((stride, step))
        stride, rest = stride * step, rest // step
    return core, [(1, fsdp)] + sizes


def plan_of(dp, fsdp, rows):
    core, links = dims_of(dp, fsdp)
    tiles = rows // TILE
    if len(links) != 3 or tiles < 3:
        return [(0, rows, [core] + links)]
    y, x, z = links
    outer = max(1, (tiles * 3 + 4) // 8)
    inner = tiles - 2 * outer
    orders = [[core, y, x, z], [core, z, y, x], [core, x, z, y]]
    plan, start = [], 0
    for count, order in zip((outer, inner, outer), orders):
        plan.append((start * TILE, count * TILE, order))
        start += count
    return plan


def prod_of(order):
    total = 1
    for _, size in order:
        total *= size
    return total


def coord(me, dim):
    return lax.rem(me // dim[0], dim[1])


def moved(slab, dim, old, new):
    return slab + (new - old) * dim[0]


def spread(slab, me, dims, k):
    for dim in reversed(dims):
        slab = moved(slab, dim, coord(me, dim), lax.rem(k, dim[1]))
        k = k // dim[1]
    return slab


def whoami(fsdp):
    return lax.axis_index("dp") * fsdp + lax.axis_index("fsdp")


def place(number, fsdp):
    return (number // fsdp, lax.rem(number, fsdp))


def greet(me, dims, fsdp):
    barrier = pltpu.get_barrier_semaphore()
    count = 0
    for dim in dims:
        mine = coord(me, dim)
        for r in range(dim[1] - 1):
            peer = moved(me, dim, mine, lax.rem(mine + 1 + r, dim[1]))
            pl.semaphore_signal(barrier, inc=1, device_id=place(peer, fsdp), device_id_type=MESH)
            count += 1
    pl.semaphore_wait(barrier, count)


def gather_kernel(dp, fsdp, plan, x_ref, out_ref, send_sem, recv_sem, own_sem):
    me = whoami(fsdp)
    greet(me, plan[0][2], fsdp)
    own = pltpu.make_async_copy(x_ref, out_ref.at[me], own_sem)
    own.start()

    def copy_of(band, slab, slot, peer, first):
        start, rows, _ = plan[band]
        here = out_ref.at[slab, pl.ds(start, rows), :]
        source = x_ref.at[pl.ds(start, rows), :] if first else here
        return pltpu.make_async_remote_copy(
            src_ref=source,
            dst_ref=here,
            send_sem=send_sem.at[band, slot],
            recv_sem=recv_sem.at[band, slab],
            device_id=place(peer, fsdp),
            device_id_type=MESH,
        )

    bases = []
    for _, _, order in plan:
        tree = order[1:] + order[:1]
        base, at = {}, 0
        for i in range(-1, len(tree)):
            arrivals = 1 if i < 0 else prod_of(tree[:i]) * (tree[i][1] - 1)
            for j in range(i + 1, len(tree)):
                base[i, j] = at
                at += arrivals * (tree[j][1] - 1)
        bases.append(base)
    depth = len(plan[0][2])
    for i in range(-1, depth):
        for band in range(len(plan)):
            order = plan[band][2]
            tree = order[1:] + order[:1]

            def sends(slab, k, act, i=i, band=band, tree=tree):
                for j in range(i + 1, depth):
                    dim = tree[j]
                    mine = coord(me, dim)
                    for r in range(dim[1] - 1):
                        peer = moved(me, dim, mine, lax.rem(mine + 1 + r, dim[1]))
                        slot = bases[band][i, j] + k * (dim[1] - 1) + r
                        act(copy_of(band, slab, slot, peer, i < 0))

            if i < 0:
                sends(me, 0, lambda c: c.start())
                continue
            dim = tree[i]
            mine = coord(me, dim)

            def arrived(k, _, i=i, band=band, tree=tree, dim=dim, mine=mine, sends=sends):
                gap = dim[1] - 1
                peer = moved(me, dim, mine, lax.rem(mine + 1 + lax.rem(k, gap), dim[1]))
                slab = spread(peer, me, tree[:i], k // gap)
                copy_of(band, slab, 0, peer, False).wait_recv()
                sends(slab, k, lambda c: c.start())
                return 0

            lax.fori_loop(0, prod_of(tree[:i]) * (dim[1] - 1), arrived, 0)
    own.wait()
    for band in range(len(plan)):
        peer = moved(me, plan[band][2][0], coord(me, plan[band][2][0]), 1 - coord(me, plan[band][2][0]))

        def sent(slot, _, band=band, peer=peer):
            copy_of(band, me, slot, peer, True).wait_send()
            return 0

        lax.fori_loop(0, dp * fsdp - 1, sent, 0)


def gather(dp, fsdp, shard):
    rows, width = shard.shape
    plan = plan_of(dp, fsdp, rows)
    n = dp * fsdp
    return pl.pallas_call(
        partial(gather_kernel, dp, fsdp, plan),
        out_shape=jax.ShapeDtypeStruct((n, rows, width), shard.dtype),
        in_specs=[pl.BlockSpec(memory_space=pl.ANY)],
        out_specs=pl.BlockSpec(memory_space=pl.ANY),
        scratch_shapes=[
            pltpu.SemaphoreType.DMA((len(plan), n)),
            pltpu.SemaphoreType.DMA((len(plan), n)),
            pltpu.SemaphoreType.DMA,
        ],
        compiler_params=pltpu.CompilerParams(collective_id=0, has_side_effects=True),
        name="gather_params",
    )(shard)


def sum_kernel(dp, fsdp, plan, x_ref, out_ref, *scratch):
    bands = len(plan)
    kept, held = scratch[:bands], scratch[bands : 2 * bands]
    send_sem, recv_sem, own_sem = scratch[2 * bands :]
    me = whoami(fsdp)
    greet(me, plan[0][2], fsdp)
    f32 = jnp.float32
    depth = len(plan[0][2])
    bases = []
    for _, _, order in plan:
        base, at = [], 0
        for i in range(depth):
            base.append(at)
            at += prod_of(order[i + 1 :]) * (order[i][1] - 1)
        bases.append(base)

    def sending(band, i, source, r, rest):
        dim = plan[band][2][i]
        mine = coord(me, dim)
        gap = dim[1] - 1
        there = lax.rem(mine + 1 + r, dim[1])
        back = lax.rem(mine - there - 1 + 2 * dim[1], dim[1])
        slot = bases[band][i] + rest * gap + back
        return pltpu.make_async_remote_copy(
            src_ref=source,
            dst_ref=held[band].at[slot],
            send_sem=send_sem.at[band, bases[band][i] + rest * gap + r],
            recv_sem=recv_sem.at[band, slot],
            device_id=place(moved(me, dim, mine, there), fsdp),
            device_id_type=MESH,
        )

    def own_copy(band, index):
        start, rows, order = plan[band]
        slab = spread(me, me, order[1:], index)
        return pltpu.make_async_copy(
            x_ref.at[slab, pl.ds(start, rows), :], kept[band].at[index], own_sem.at[band, index]
        )

    def walk(band, i, visit):
        order = plan[band][2]
        if i == depth - 1:
            visit(0, 0, 0)
            return
        dim = order[i + 1]
        inner = prod_of(order[i + 2 :])
        for r in range(dim[1]):
            at = lax.rem(coord(me, dim) + 1 + r, dim[1])

            def one(rest, _, r=r, at=at):
                visit(r, rest, at * inner + rest)
                return 0

            lax.fori_loop(0, inner, one, 0)

    for band in range(bands):
        start, rows, order = plan[band]
        core = order[0]
        mine = coord(me, core)

        def begin(r, rest, index, band=band, start=start, rows=rows, order=order, core=core, mine=mine):
            slab = moved(spread(me, me, order[1:], index), core, mine, lax.rem(mine + 1, core[1]))
            sending(band, 0, x_ref.at[slab, pl.ds(start, rows), :], 0, index).start()
            own_copy(band, index).start()

        walk(band, 0, begin)
    for i in range(depth):
        for band in range(bands):
            start, rows, order = plan[band]
            gap = order[i][1] - 1
            where = 0
            for dim in order[1 : i + 1]:
                where = where * dim[1] + coord(me, dim)
            where = where * prod_of(order[i + 1 :])

            def visit(r, rest, index, i=i, band=band, start=start, rows=rows, order=order, gap=gap, where=where):
                if i == 0:
                    own_copy(band, index).wait()
                total = kept[band][where + index].astype(f32)
                for q in range(gap):
                    slot = bases[band][i] + index * gap + q
                    pltpu.make_async_remote_copy(
                        src_ref=held[band].at[slot],
                        dst_ref=held[band].at[slot],
                        send_sem=send_sem.at[band, 0],
                        recv_sem=recv_sem.at[band, slot],
                        device_id=place(moved(me, order[0], coord(me, order[0]), 1 - coord(me, order[0])), fsdp),
                        device_id_type=MESH,
                    ).wait_recv()
                    total = total + held[band][slot].astype(f32)
                if i == depth - 1:
                    out_ref[start : start + rows, :] = total
                    return
                kept[band][where + index] = total.astype(kept[band].dtype)
                if r < order[i + 1][1] - 1:
                    sending(band, i + 1, kept[band].at[where + index], r, rest).start()

            walk(band, i, visit)
    for band in range(bands):
        start, rows, order = plan[band]

        def sent(slot, _, band=band):
            core = plan[band][2][0]
            pltpu.make_async_remote_copy(
                src_ref=held[band].at[0],
                dst_ref=held[band].at[0],
                send_sem=send_sem.at[band, slot],
                recv_sem=recv_sem.at[band, 0],
                device_id=place(moved(me, core, coord(me, core), 1 - coord(me, core)), fsdp),
                device_id_type=MESH,
            ).wait_send()
            return 0

        lax.fori_loop(0, dp * fsdp - 1, sent, 0)


def sum_shards(dp, fsdp, terms):
    n, rows, width = terms.shape
    plan = plan_of(dp, fsdp, rows)
    return pl.pallas_call(
        partial(sum_kernel, dp, fsdp, plan),
        out_shape=jax.ShapeDtypeStruct((rows, width), jnp.float32),
        in_specs=[pl.BlockSpec(memory_space=pl.ANY)],
        out_specs=pl.BlockSpec(memory_space=pltpu.VMEM),
        scratch_shapes=[pltpu.VMEM((n // 2, band[1], width), terms.dtype) for band in plan]
        + [pltpu.VMEM((n - 1, band[1], width), terms.dtype) for band in plan]
        + [
            pltpu.SemaphoreType.DMA((len(plan), n)),
            pltpu.SemaphoreType.DMA((len(plan), n)),
            pltpu.SemaphoreType.DMA((len(plan), n // 2)),
        ],
        compiler_params=pltpu.CompilerParams(
            collective_id=1, has_side_effects=True, vmem_limit_bytes=56 * 1024 * 1024
        ),
        name="sum_grads",
    )(terms)


PARAM_NAMES = [
    "query_weight",
    "key_weight",
    "value_weight",
    "query_bias",
    "value_bias",
    "out_weight",
    "out_bias",
    "first_gain",
    "first_shift",
    "up_weight",
    "up_bias",
    "down_weight",
    "down_bias",
    "second_gain",
    "second_shift",
]
VECTORS = [name for name in PARAM_NAMES if not name.endswith("_weight")]

def normalize(rows, gain, shift):
    centred = rows - jnp.mean(rows, axis=-1, keepdims=True)
    scale = lax.rsqrt(jnp.mean(centred * centred, axis=-1, keepdims=True) + 1e-06)
    normed = centred * scale
    return (normed * gain + shift, normed, scale)


def norm_back(grad, normed, scale, gain):
    scaled = grad * gain
    return scale * (
        scaled
        - jnp.mean(scaled, axis=-1, keepdims=True)
        - normed * jnp.mean(scaled * normed, axis=-1, keepdims=True)
    )


def rowdot(left, right):
    return jnp.einsum("ti,to->io", left, right, preferred_element_type=jnp.float32)


def backdot(left, right):
    return jnp.einsum("to,io->ti", left, right, preferred_element_type=jnp.float32)


def on_device(
    dp,
    fsdp,
    tokens,
    query_weight,
    key_weight,
    value_weight,
    query_bias,
    value_bias,
    out_weight,
    out_bias,
    first_gain,
    first_shift,
    up_weight,
    up_bias,
    down_weight,
    down_bias,
    second_gain,
    second_shift,
    segment_ids,
    out_grad,
):
    bf16 = jnp.bfloat16
    width = tokens.shape[1]
    n = dp * fsdp
    given = dict(
        query_bias=query_bias,
        value_bias=value_bias,
        out_bias=out_bias,
        first_gain=first_gain,
        first_shift=first_shift,
        up_bias=up_bias,
        down_bias=down_bias,
        second_gain=second_gain,
        second_shift=second_shift,
    )
    part = query_weight.shape[0]
    wide = up_weight.shape[1] // width
    tall = down_weight.shape[0]
    flat = jnp.concatenate([given[name] for name in VECTORS])
    used = (4 + wide) * part + tall
    lines = -(-flat.shape[0] // width)
    total_rows = -(-(used + lines) // TILE) * TILE
    flat = jnp.pad(flat, (0, (total_rows - used) * width - flat.shape[0])).reshape(-1, width)
    shard = jnp.concatenate(
        [query_weight, key_weight, value_weight, out_weight]
        + [up_weight[:, j * width : (j + 1) * width] for j in range(wide)]
        + [down_weight, flat],
        axis=0,
    )
    slabs = gather(dp, fsdp, shard)

    def matrix(k):
        return slabs[:, k * part : (k + 1) * part, :].reshape(n * part, width)

    params = dict(
        query_weight=matrix(0),
        key_weight=matrix(1),
        value_weight=matrix(2),
        out_weight=matrix(3),
        up_weight=jnp.concatenate([matrix(4 + j) for j in range(wide)], axis=1),
        down_weight=slabs[:, (4 + wide) * part : used, :].reshape(n * tall, width),
    )
    flat = slabs[:, used : used + lines, :].reshape(n, lines * width)
    at = 0
    for name in VECTORS:
        count = given[name].shape[0]
        params[name] = flat[:, at : at + count].reshape(-1)
        at += count
    length = tokens.shape[0]
    width = tokens.shape[1]
    heads = width // HD
    f32 = jnp.float32
    bf16 = jnp.bfloat16

    def split_heads(rows):
        return rows.reshape(length, heads, HD)

    query = (
        jnp.dot(tokens, params["query_weight"], preferred_element_type=f32)
        + params["query_bias"].astype(f32)
    ).astype(bf16)
    keys = jnp.dot(tokens, params["key_weight"], preferred_element_type=f32).astype(bf16)
    values = (
        jnp.dot(tokens, params["value_weight"], preferred_element_type=f32)
        + params["value_bias"].astype(f32)
    ).astype(bf16)
    same = (segment_ids[0][:, None] == segment_ids[0][None, :])[None]
    scores = (
        jnp.einsum(
            "qhd,khd->hqk", split_heads(query), split_heads(keys), preferred_element_type=f32
        )
        * 0.125
    )
    masked = jnp.where(same, scores, -1e30)
    top = jnp.max(masked, axis=-1, keepdims=True)
    expo = jnp.exp(masked - top)
    total = jnp.sum(expo, axis=-1, keepdims=True)
    probs = expo / total
    probs_low = probs.astype(bf16)
    attended = (
        jnp.einsum("hqk,khd->qhd", probs_low, split_heads(values), preferred_element_type=f32)
        .reshape(length, width)
        .astype(bf16)
    )
    branch = jnp.dot(attended, params["out_weight"], preferred_element_type=f32) + params[
        "out_bias"
    ].astype(f32)
    gain_first = params["first_gain"].astype(f32)
    first, normed_first, scale_first = normalize(
        tokens.astype(f32) + branch, gain_first, params["first_shift"].astype(f32)
    )
    first_low = first.astype(bf16)
    hidden = jnp.dot(first_low, params["up_weight"], preferred_element_type=f32) + params[
        "up_bias"
    ].astype(f32)
    active_full, gelu_back = jax.vjp(partial(jax.nn.gelu, approximate=False), hidden)
    active = active_full.astype(bf16)
    second_in = (
        first
        + jnp.dot(active, params["down_weight"], preferred_element_type=f32)
        + params["down_bias"].astype(f32)
    )
    gain_second = params["second_gain"].astype(f32)
    result, normed_second, scale_second = normalize(
        second_in, gain_second, params["second_shift"].astype(f32)
    )
    layer_output = result.astype(bf16)
    grad_out = out_grad.astype(f32)
    grads = {}
    grads["second_gain"] = jnp.sum(grad_out * normed_second, axis=0)
    grads["second_shift"] = jnp.sum(grad_out, axis=0)
    d_second = norm_back(grad_out, normed_second, scale_second, gain_second)
    d_down = d_second.astype(bf16)
    grads["down_bias"] = jnp.sum(d_down.astype(f32), axis=0)
    grads["down_weight"] = rowdot(active, d_down)
    d_hidden = gelu_back(backdot(d_down, params["down_weight"]))[0].astype(bf16)
    grads["up_bias"] = jnp.sum(d_hidden.astype(f32), axis=0)
    grads["up_weight"] = rowdot(first_low, d_hidden)
    d_first = d_second + backdot(d_hidden, params["up_weight"])
    grads["first_gain"] = jnp.sum(d_first * normed_first, axis=0)
    grads["first_shift"] = jnp.sum(d_first, axis=0)
    d_branch_full = norm_back(d_first, normed_first, scale_first, gain_first)
    d_branch = d_branch_full.astype(bf16)
    grads["out_bias"] = jnp.sum(d_branch.astype(f32), axis=0)
    grads["out_weight"] = rowdot(attended, d_branch)
    d_attended = split_heads(backdot(d_branch, params["out_weight"]).astype(bf16))
    d_probs = jnp.einsum(
        "qhd,khd->hqk", d_attended, split_heads(values), preferred_element_type=f32
    )
    d_scores = (probs * (d_probs - jnp.sum(d_probs * probs, axis=-1, keepdims=True))).astype(bf16)
    d_query = (
        (
            jnp.einsum("hqk,khd->qhd", d_scores, split_heads(keys), preferred_element_type=f32)
            * 0.125
        )
        .reshape(length, width)
        .astype(bf16)
    )
    d_keys = (
        (
            jnp.einsum("hqk,qhd->khd", d_scores, split_heads(query), preferred_element_type=f32)
            * 0.125
        )
        .reshape(length, width)
        .astype(bf16)
    )
    d_values = (
        jnp.einsum("hqk,qhd->khd", probs_low, d_attended, preferred_element_type=f32)
        .reshape(length, width)
        .astype(bf16)
    )
    grads["query_weight"] = rowdot(tokens, d_query)
    grads["key_weight"] = rowdot(tokens, d_keys)
    grads["value_weight"] = rowdot(tokens, d_values)
    grads["query_bias"] = jnp.sum(d_query.astype(f32), axis=0)
    grads["value_bias"] = jnp.sum(d_values.astype(f32), axis=0)
    input_grad = (
        d_branch_full
        + backdot(d_query, params["query_weight"])
        + backdot(d_keys, params["key_weight"])
        + backdot(d_values, params["value_weight"])
    )
    def by_owner(value):
        return value.astype(bf16).reshape(n, -1, width)

    flat = jnp.concatenate(
        [grads[name].astype(bf16).reshape(n, -1) for name in VECTORS], axis=1
    )
    flat = jnp.pad(flat, ((0, 0), (0, (total_rows - used) * width - flat.shape[1])))
    up = grads["up_weight"].astype(bf16)
    terms = jnp.concatenate(
        [by_owner(grads[name + "_weight"]) for name in ("query", "key", "value", "out")]
        + [by_owner(up[:, j * width : (j + 1) * width]) for j in range(wide)]
        + [by_owner(grads["down_weight"]), flat.reshape(n, -1, width)],
        axis=1,
    )
    sums = sum_shards(dp, fsdp, terms)
    owned = {}
    for k, name in enumerate(("query", "key", "value", "out")):
        owned[name + "_weight"] = sums[k * part : (k + 1) * part]
    owned["up_weight"] = jnp.concatenate(
        [sums[(4 + j) * part : (5 + j) * part] for j in range(wide)], axis=1
    )
    owned["down_weight"] = sums[(4 + wide) * part : used]
    flat = sums[used : used + lines].reshape(-1)
    at = 0
    for name in VECTORS:
        count = given[name].shape[0]
        owned[name] = flat[at : at + count]
        at += count
    return tuple([layer_output, input_grad] + [owned[name] for name in PARAM_NAMES])


def solution(mesh):
    in_specs = (
        P(("dp", "fsdp"), None),
        P(("dp", "fsdp"), None),
        P(("dp", "fsdp"), None),
        P(("dp", "fsdp"), None),
        P(("dp", "fsdp")),
        P(("dp", "fsdp")),
        P(("dp", "fsdp"), None),
        P(("dp", "fsdp")),
        P(("dp", "fsdp")),
        P(("dp", "fsdp")),
        P(("dp", "fsdp"), None),
        P(("dp", "fsdp")),
        P(("dp", "fsdp"), None),
        P(("dp", "fsdp")),
        P(("dp", "fsdp")),
        P(("dp", "fsdp")),
        P(("dp", "fsdp"), None),
        P(("dp", "fsdp"), None),
    )
    out_specs = (
        P(("dp", "fsdp"), None),
        P(("dp", "fsdp"), None),
        P(("dp", "fsdp"), None),
        P(("dp", "fsdp"), None),
        P(("dp", "fsdp"), None),
        P(("dp", "fsdp")),
        P(("dp", "fsdp")),
        P(("dp", "fsdp"), None),
        P(("dp", "fsdp")),
        P(("dp", "fsdp")),
        P(("dp", "fsdp")),
        P(("dp", "fsdp"), None),
        P(("dp", "fsdp")),
        P(("dp", "fsdp"), None),
        P(("dp", "fsdp")),
        P(("dp", "fsdp")),
        P(("dp", "fsdp")),
    )
    return jax.shard_map(
        partial(on_device, mesh.shape["dp"], mesh.shape["fsdp"]),
        mesh=mesh,
        in_specs=in_specs,
        out_specs=out_specs,
        check_vma=False,
    )
```

```python
from functools import partial

import jax
import jax.numpy as jnp
from jax import lax
from jax.experimental import pallas as pl
from jax.experimental.pallas import tpu as pltpu
from jax.sharding import PartitionSpec as P

HD = 64
MESH = pl.DeviceIdType.MESH
TILE = 16


def dims_of(dp, fsdp):
    core = (fsdp, 2 if dp % 2 == 0 else 1)
    rest, stride = dp // core[1], fsdp * core[1]
    sizes = []
    while rest > 1:
        step = 2 if rest % 4 else 4
        if not sizes and rest % 2 == 0:
            step = 2
        if rest % step:
            step = rest
        sizes.append((stride, step))
        stride, rest = stride * step, rest // step
    return core, [(1, fsdp)] + sizes


def plan_of(dp, fsdp, rows):
    core, links = dims_of(dp, fsdp)
    tiles = rows // TILE
    if len(links) != 3 or tiles < 2:
        return [(0, rows, [core] + links)]
    y, x, z = links
    most = max(1, min(tiles - 1, (tiles * 7 + 5) // 11))
    orders = [[core, y, x, z], [core, x, z, y]]
    plan, start = [], 0
    for count, order in zip((most, tiles - most), orders):
        plan.append((start * TILE, count * TILE, order))
        start += count
    return plan


def prod_of(order):
    total = 1
    for _, size in order:
        total *= size
    return total


def coord(me, dim):
    return lax.rem(me // dim[0], dim[1])


def moved(slab, dim, old, new):
    return slab + (new - old) * dim[0]


def spread(slab, me, dims, k):
    for dim in reversed(dims):
        slab = moved(slab, dim, coord(me, dim), lax.rem(k, dim[1]))
        k = k // dim[1]
    return slab


def whoami(fsdp):
    return lax.axis_index("dp") * fsdp + lax.axis_index("fsdp")


def place(number, fsdp):
    return (number // fsdp, lax.rem(number, fsdp))


def greet(me, dims, fsdp):
    barrier = pltpu.get_barrier_semaphore()
    count = 0
    for dim in dims:
        mine = coord(me, dim)
        for r in range(dim[1] - 1):
            peer = moved(me, dim, mine, lax.rem(mine + 1 + r, dim[1]))
            pl.semaphore_signal(barrier, inc=1, device_id=place(peer, fsdp), device_id_type=MESH)
            count += 1
    pl.semaphore_wait(barrier, count)


def gather_kernel(dp, fsdp, plan, *refs):
    *parts, out_ref, x_ref, send_sem, recv_sem, own_sem = refs
    me = whoami(fsdp)
    blocks, width = [], x_ref.shape[1]
    for ref in parts:
        for j in range(ref.shape[1] // width):
            blocks.append(ref[:, j * width : (j + 1) * width].astype(jnp.float32))
    x_ref[...] = jnp.concatenate(blocks, axis=0).astype(x_ref.dtype)
    greet(me, plan[0][2], fsdp)
    own = pltpu.make_async_copy(x_ref, out_ref.at[me], own_sem)
    own.start()

    def copy_of(band, slab, slot, peer, first):
        start, rows, _ = plan[band]
        here = out_ref.at[slab, pl.ds(start, rows), :]
        source = x_ref.at[pl.ds(start, rows), :] if first else here
        return pltpu.make_async_remote_copy(
            src_ref=source,
            dst_ref=here,
            send_sem=send_sem.at[band, slot],
            recv_sem=recv_sem.at[band, slab],
            device_id=place(peer, fsdp),
            device_id_type=MESH,
        )

    bases = []
    for _, _, order in plan:
        tree = order[:0:-1] + order[:1]
        base, at = {}, 0
        for i in range(-1, len(tree)):
            arrivals = 1 if i < 0 else prod_of(tree[:i]) * (tree[i][1] - 1)
            for j in range(i + 1, len(tree)):
                base[i, j] = at
                at += arrivals * (tree[j][1] - 1)
        bases.append(base)
    depth = len(plan[0][2])
    for i in range(-1, depth):
        for band in range(len(plan)):
            order = plan[band][2]
            tree = order[:0:-1] + order[:1]

            def sends(slab, k, act, i=i, band=band, tree=tree):
                for j in range(i + 1, depth):
                    dim = tree[j]
                    mine = coord(me, dim)
                    for r in range(dim[1] - 1):
                        peer = moved(me, dim, mine, lax.rem(mine + 1 + r, dim[1]))
                        slot = bases[band][i, j] + k * (dim[1] - 1) + r
                        act(copy_of(band, slab, slot, peer, i < 0))

            if i < 0:
                sends(me, 0, lambda c: c.start())
                continue
            dim = tree[i]
            mine = coord(me, dim)

            def arrived(k, _, i=i, band=band, tree=tree, dim=dim, mine=mine, sends=sends):
                gap = dim[1] - 1
                peer = moved(me, dim, mine, lax.rem(mine + 1 + lax.rem(k, gap), dim[1]))
                slab = spread(peer, me, tree[:i], k // gap)
                copy_of(band, slab, 0, peer, False).wait_recv()
                sends(slab, k, lambda c: c.start())
                return 0

            lax.fori_loop(0, prod_of(tree[:i]) * (dim[1] - 1), arrived, 0)
    own.wait()
    for band in range(len(plan)):
        peer = moved(me, plan[band][2][0], coord(me, plan[band][2][0]), 1 - coord(me, plan[band][2][0]))

        def sent(slot, _, band=band, peer=peer):
            copy_of(band, me, slot, peer, True).wait_send()
            return 0

        lax.fori_loop(0, dp * fsdp - 1, sent, 0)


def gather(dp, fsdp, parts, rows, width):
    plan = plan_of(dp, fsdp, rows)
    n = dp * fsdp
    return pl.pallas_call(
        partial(gather_kernel, dp, fsdp, plan),
        out_shape=jax.ShapeDtypeStruct((n, rows, width), parts[0].dtype),
        in_specs=[pl.BlockSpec(memory_space=pltpu.VMEM)] * len(parts),
        out_specs=pl.BlockSpec(memory_space=pl.ANY),
        scratch_shapes=[
            pltpu.VMEM((rows, width), parts[0].dtype),
            pltpu.SemaphoreType.DMA((len(plan), n)),
            pltpu.SemaphoreType.DMA((len(plan), n)),
            pltpu.SemaphoreType.DMA,
        ],
        compiler_params=pltpu.CompilerParams(collective_id=0, has_side_effects=True, vmem_limit_bytes=6 * 1024 * 1024),
        name="gather_params",
    )(*parts)


def sum_kernel(dp, fsdp, plan, x_ref, out_ref, *scratch):
    bands = len(plan)
    kept, held = scratch[:bands], scratch[bands : 2 * bands]
    send_sem, recv_sem, own_sem = scratch[2 * bands :]
    me = whoami(fsdp)
    greet(me, plan[0][2], fsdp)
    f32 = jnp.float32
    depth = len(plan[0][2])
    bases = []
    for _, _, order in plan:
        base, at = [], 0
        for i in range(depth):
            base.append(at)
            at += prod_of(order[i + 1 :]) * (order[i][1] - 1)
        bases.append(base)

    def sending(band, i, source, r, rest):
        dim = plan[band][2][i]
        mine = coord(me, dim)
        gap = dim[1] - 1
        there = lax.rem(mine + 1 + r, dim[1])
        back = lax.rem(mine - there - 1 + 2 * dim[1], dim[1])
        slot = bases[band][i] + rest * gap + back
        return pltpu.make_async_remote_copy(
            src_ref=source,
            dst_ref=held[band].at[slot],
            send_sem=send_sem.at[band, bases[band][i] + rest * gap + r],
            recv_sem=recv_sem.at[band, slot],
            device_id=place(moved(me, dim, mine, there), fsdp),
            device_id_type=MESH,
        )

    def own_copy(band, index):
        start, rows, order = plan[band]
        slab = spread(me, me, order[1:], index)
        return pltpu.make_async_copy(
            x_ref.at[slab, pl.ds(start, rows), :], kept[band].at[index], own_sem.at[band, index]
        )

    def walk(band, i, visit):
        order = plan[band][2]
        if i == depth - 1:
            visit(0, 0, 0)
            return
        dim = order[i + 1]
        inner = prod_of(order[i + 2 :])
        for r in range(dim[1]):
            at = lax.rem(coord(me, dim) + 1 + r, dim[1])

            def one(rest, _, r=r, at=at):
                visit(r, rest, at * inner + rest)
                return 0

            lax.fori_loop(0, inner, one, 0)

    for band in range(bands):
        start, rows, order = plan[band]
        core = order[0]
        mine = coord(me, core)

        def begin(r, rest, index, band=band, start=start, rows=rows, order=order, core=core, mine=mine):
            slab = moved(spread(me, me, order[1:], index), core, mine, lax.rem(mine + 1, core[1]))
            sending(band, 0, x_ref.at[slab, pl.ds(start, rows), :], 0, index).start()
            own_copy(band, index).start()

        walk(band, 0, begin)
    for i in range(depth):
        for band in range(bands):
            start, rows, order = plan[band]
            gap = order[i][1] - 1
            where = 0
            for dim in order[1 : i + 1]:
                where = where * dim[1] + coord(me, dim)
            where = where * prod_of(order[i + 1 :])

            def visit(r, rest, index, i=i, band=band, start=start, rows=rows, order=order, gap=gap, where=where):
                if i == 0:
                    own_copy(band, index).wait()
                total = kept[band][where + index].astype(f32)
                for q in range(gap):
                    slot = bases[band][i] + index * gap + q
                    pltpu.make_async_remote_copy(
                        src_ref=held[band].at[slot],
                        dst_ref=held[band].at[slot],
                        send_sem=send_sem.at[band, 0],
                        recv_sem=recv_sem.at[band, slot],
                        device_id=place(moved(me, order[0], coord(me, order[0]), 1 - coord(me, order[0])), fsdp),
                        device_id_type=MESH,
                    ).wait_recv()
                    total = total + held[band][slot].astype(f32)
                if i == depth - 1:
                    out_ref[start : start + rows, :] = total
                    return
                kept[band][where + index] = total.astype(kept[band].dtype)
                if r < order[i + 1][1] - 1:
                    sending(band, i + 1, kept[band].at[where + index], r, rest).start()

            walk(band, i, visit)
    for band in range(bands):
        start, rows, order = plan[band]

        def sent(slot, _, band=band):
            core = plan[band][2][0]
            pltpu.make_async_remote_copy(
                src_ref=held[band].at[0],
                dst_ref=held[band].at[0],
                send_sem=send_sem.at[band, slot],
                recv_sem=recv_sem.at[band, 0],
                device_id=place(moved(me, core, coord(me, core), 1 - coord(me, core)), fsdp),
                device_id_type=MESH,
            ).wait_send()
            return 0

        lax.fori_loop(0, dp * fsdp - 1, sent, 0)


def sum_shards(dp, fsdp, terms):
    n, rows, width = terms.shape
    plan = plan_of(dp, fsdp, rows)
    return pl.pallas_call(
        partial(sum_kernel, dp, fsdp, plan),
        out_shape=jax.ShapeDtypeStruct((rows, width), jnp.float32),
        in_specs=[pl.BlockSpec(memory_space=pl.ANY)],
        out_specs=pl.BlockSpec(memory_space=pltpu.VMEM),
        scratch_shapes=[pltpu.VMEM((n // 2, band[1], width), terms.dtype) for band in plan]
        + [pltpu.VMEM((n - 1, band[1], width), terms.dtype) for band in plan]
        + [
            pltpu.SemaphoreType.DMA((len(plan), n)),
            pltpu.SemaphoreType.DMA((len(plan), n)),
            pltpu.SemaphoreType.DMA((len(plan), n // 2)),
        ],
        compiler_params=pltpu.CompilerParams(
            collective_id=1, has_side_effects=True, vmem_limit_bytes=28 * 1024 * 1024 if n <= 64 else 56 * 1024 * 1024
        ),
        name="sum_grads",
    )(terms)


PARAM_NAMES = [
    "query_weight",
    "key_weight",
    "value_weight",
    "query_bias",
    "value_bias",
    "out_weight",
    "out_bias",
    "first_gain",
    "first_shift",
    "up_weight",
    "up_bias",
    "down_weight",
    "down_bias",
    "second_gain",
    "second_shift",
]
VECTORS = [name for name in PARAM_NAMES if not name.endswith("_weight")]

def normalize(rows, gain, shift):
    centred = rows - jnp.mean(rows, axis=-1, keepdims=True)
    scale = lax.rsqrt(jnp.mean(centred * centred, axis=-1, keepdims=True) + 1e-06)
    normed = centred * scale
    return (normed * gain + shift, normed, scale)


def norm_back(grad, normed, scale, gain):
    scaled = grad * gain
    return scale * (
        scaled
        - jnp.mean(scaled, axis=-1, keepdims=True)
        - normed * jnp.mean(scaled * normed, axis=-1, keepdims=True)
    )


def rowdot(left, right):
    return jnp.einsum("ti,to->io", left, right, preferred_element_type=jnp.float32)


def backdot(left, right):
    return jnp.einsum("to,io->ti", left, right, preferred_element_type=jnp.float32)


def on_device(
    dp,
    fsdp,
    tokens,
    query_weight,
    key_weight,
    value_weight,
    query_bias,
    value_bias,
    out_weight,
    out_bias,
    first_gain,
    first_shift,
    up_weight,
    up_bias,
    down_weight,
    down_bias,
    second_gain,
    second_shift,
    segment_ids,
    out_grad,
):
    bf16 = jnp.bfloat16
    width = tokens.shape[1]
    n = dp * fsdp
    given = dict(
        query_bias=query_bias,
        value_bias=value_bias,
        out_bias=out_bias,
        first_gain=first_gain,
        first_shift=first_shift,
        up_bias=up_bias,
        down_bias=down_bias,
        second_gain=second_gain,
        second_shift=second_shift,
    )
    part = query_weight.shape[0]
    wide = up_weight.shape[1] // width
    tall = down_weight.shape[0]
    used = (4 + wide) * part + tall
    lines = len(VECTORS)
    total_rows = -(-(used + lines) // TILE) * TILE
    row = lax.broadcasted_iota(jnp.int32, (total_rows - used, width), 0)
    flat = jnp.zeros((total_rows - used, width), jnp.float32)
    for k, name in enumerate(VECTORS):
        padded = jnp.pad(given[name].astype(jnp.float32), (0, width - given[name].shape[0]))
        flat = jnp.where(row == k, padded[None, :], flat)
    flat = flat.astype(bf16)
    parts = [query_weight, key_weight, value_weight, out_weight, up_weight, down_weight, flat]
    if part % 8 or tall % 8:
        wides = [up_weight[:, j * width : (j + 1) * width] for j in range(wide)]
        parts = [jnp.concatenate(parts[:4] + wides + parts[5:], axis=0)]
    slabs = gather(dp, fsdp, parts, total_rows, width)

    def matrix(k):
        return slabs[:, k * part : (k + 1) * part, :].reshape(n * part, width)

    params = dict(
        query_weight=matrix(0),
        key_weight=matrix(1),
        value_weight=matrix(2),
        out_weight=matrix(3),
        up_weight=jnp.concatenate([matrix(4 + j) for j in range(wide)], axis=1),
        down_weight=slabs[:, (4 + wide) * part : used, :].reshape(n * tall, width),
    )
    for k, name in enumerate(VECTORS):
        params[name] = slabs[:, used + k, : given[name].shape[0]].reshape(-1)
    length = tokens.shape[0]
    width = tokens.shape[1]
    heads = width // HD
    f32 = jnp.float32
    bf16 = jnp.bfloat16

    def split_heads(rows):
        return rows.reshape(length, heads, HD)

    query = (
        jnp.dot(tokens, params["query_weight"], preferred_element_type=f32)
        + params["query_bias"].astype(f32)
    ).astype(bf16)
    keys = jnp.dot(tokens, params["key_weight"], preferred_element_type=f32).astype(bf16)
    values = (
        jnp.dot(tokens, params["value_weight"], preferred_element_type=f32)
        + params["value_bias"].astype(f32)
    ).astype(bf16)
    same = (segment_ids[0][:, None] == segment_ids[0][None, :])[None]
    scores = (
        jnp.einsum(
            "qhd,khd->hqk", split_heads(query), split_heads(keys), preferred_element_type=f32
        )
        * 0.125
    )
    masked = jnp.where(same, scores, -1e30)
    top = jnp.max(masked, axis=-1, keepdims=True)
    expo = jnp.exp(masked - top)
    total = jnp.sum(expo, axis=-1, keepdims=True)
    probs = expo / total
    probs_low = probs.astype(bf16)
    attended = (
        jnp.einsum("hqk,khd->qhd", probs_low, split_heads(values), preferred_element_type=f32)
        .reshape(length, width)
        .astype(bf16)
    )
    branch = jnp.dot(attended, params["out_weight"], preferred_element_type=f32) + params[
        "out_bias"
    ].astype(f32)
    gain_first = params["first_gain"].astype(f32)
    first, normed_first, scale_first = normalize(
        tokens.astype(f32) + branch, gain_first, params["first_shift"].astype(f32)
    )
    first_low = first.astype(bf16)
    hidden = jnp.dot(first_low, params["up_weight"], preferred_element_type=f32) + params[
        "up_bias"
    ].astype(f32)
    active_full, gelu_back = jax.vjp(partial(jax.nn.gelu, approximate=False), hidden)
    active = active_full.astype(bf16)
    second_in = (
        first
        + jnp.dot(active, params["down_weight"], preferred_element_type=f32)
        + params["down_bias"].astype(f32)
    )
    gain_second = params["second_gain"].astype(f32)
    result, normed_second, scale_second = normalize(
        second_in, gain_second, params["second_shift"].astype(f32)
    )
    layer_output = result.astype(bf16)
    grad_out = out_grad.astype(f32)
    grads = {}
    grads["second_gain"] = jnp.sum(grad_out * normed_second, axis=0)
    grads["second_shift"] = jnp.sum(grad_out, axis=0)
    d_second = norm_back(grad_out, normed_second, scale_second, gain_second)
    d_down = d_second.astype(bf16)
    grads["down_bias"] = jnp.sum(d_down.astype(f32), axis=0)
    grads["down_weight"] = rowdot(active, d_down)
    d_hidden = gelu_back(backdot(d_down, params["down_weight"]))[0].astype(bf16)
    grads["up_bias"] = jnp.sum(d_hidden.astype(f32), axis=0)
    grads["up_weight"] = rowdot(first_low, d_hidden)
    d_first = d_second + backdot(d_hidden, params["up_weight"])
    grads["first_gain"] = jnp.sum(d_first * normed_first, axis=0)
    grads["first_shift"] = jnp.sum(d_first, axis=0)
    d_branch_full = norm_back(d_first, normed_first, scale_first, gain_first)
    d_branch = d_branch_full.astype(bf16)
    grads["out_bias"] = jnp.sum(d_branch.astype(f32), axis=0)
    grads["out_weight"] = rowdot(attended, d_branch)
    d_attended = split_heads(backdot(d_branch, params["out_weight"]).astype(bf16))
    d_probs = jnp.einsum(
        "qhd,khd->hqk", d_attended, split_heads(values), preferred_element_type=f32
    )
    d_scores = (probs * (d_probs - jnp.sum(d_probs * probs, axis=-1, keepdims=True))).astype(bf16)
    d_query = (
        (
            jnp.einsum("hqk,khd->qhd", d_scores, split_heads(keys), preferred_element_type=f32)
            * 0.125
        )
        .reshape(length, width)
        .astype(bf16)
    )
    d_keys = (
        (
            jnp.einsum("hqk,qhd->khd", d_scores, split_heads(query), preferred_element_type=f32)
            * 0.125
        )
        .reshape(length, width)
        .astype(bf16)
    )
    d_values = (
        jnp.einsum("hqk,qhd->khd", probs_low, d_attended, preferred_element_type=f32)
        .reshape(length, width)
        .astype(bf16)
    )
    grads["query_weight"] = rowdot(tokens, d_query)
    grads["key_weight"] = rowdot(tokens, d_keys)
    grads["value_weight"] = rowdot(tokens, d_values)
    grads["query_bias"] = jnp.sum(d_query.astype(f32), axis=0)
    grads["value_bias"] = jnp.sum(d_values.astype(f32), axis=0)
    input_grad = (
        d_branch_full
        + backdot(d_query, params["query_weight"])
        + backdot(d_keys, params["key_weight"])
        + backdot(d_values, params["value_weight"])
    )
    def by_owner(value):
        return value.astype(bf16).reshape(n, -1, width)

    row = lax.broadcasted_iota(jnp.int32, (n, total_rows - used, width), 1)
    flat = jnp.zeros((n, total_rows - used, width), f32)
    for k, name in enumerate(VECTORS):
        mine = grads[name].reshape(n, -1)
        mine = jnp.pad(mine, ((0, 0), (0, width - mine.shape[1])))
        flat = jnp.where(row == k, mine[:, None, :], flat)
    flat = flat.astype(bf16)
    up = grads["up_weight"].astype(bf16)
    terms = jnp.concatenate(
        [by_owner(grads[name + "_weight"]) for name in ("query", "key", "value", "out")]
        + [by_owner(up[:, j * width : (j + 1) * width]) for j in range(wide)]
        + [by_owner(grads["down_weight"]), flat],
        axis=1,
    )
    sums = sum_shards(dp, fsdp, terms)
    owned = {}
    for k, name in enumerate(("query", "key", "value", "out")):
        owned[name + "_weight"] = sums[k * part : (k + 1) * part]
    owned["up_weight"] = jnp.concatenate(
        [sums[(4 + j) * part : (5 + j) * part] for j in range(wide)], axis=1
    )
    owned["down_weight"] = sums[(4 + wide) * part : used]
    for k, name in enumerate(VECTORS):
        owned[name] = sums[used + k, : given[name].shape[0]]
    return tuple([layer_output, input_grad] + [owned[name] for name in PARAM_NAMES])


def solution(mesh):
    in_specs = (
        P(("dp", "fsdp"), None),
        P(("dp", "fsdp"), None),
        P(("dp", "fsdp"), None),
        P(("dp", "fsdp"), None),
        P(("dp", "fsdp")),
        P(("dp", "fsdp")),
        P(("dp", "fsdp"), None),
        P(("dp", "fsdp")),
        P(("dp", "fsdp")),
        P(("dp", "fsdp")),
        P(("dp", "fsdp"), None),
        P(("dp", "fsdp")),
        P(("dp", "fsdp"), None),
        P(("dp", "fsdp")),
        P(("dp", "fsdp")),
        P(("dp", "fsdp")),
        P(("dp", "fsdp"), None),
        P(("dp", "fsdp"), None),
    )
    out_specs = (
        P(("dp", "fsdp"), None),
        P(("dp", "fsdp"), None),
        P(("dp", "fsdp"), None),
        P(("dp", "fsdp"), None),
        P(("dp", "fsdp"), None),
        P(("dp", "fsdp")),
        P(("dp", "fsdp")),
        P(("dp", "fsdp"), None),
        P(("dp", "fsdp")),
        P(("dp", "fsdp")),
        P(("dp", "fsdp")),
        P(("dp", "fsdp"), None),
        P(("dp", "fsdp")),
        P(("dp", "fsdp"), None),
        P(("dp", "fsdp")),
        P(("dp", "fsdp")),
        P(("dp", "fsdp")),
    )
    return jax.shard_map(
        partial(on_device, mesh.shape["dp"], mesh.shape["fsdp"]),
        mesh=mesh,
        in_specs=in_specs,
        out_specs=out_specs,
        check_vma=False,
    )
```

```python
from functools import partial

import jax
import jax.numpy as jnp
from jax import lax
from jax.experimental import pallas as pl
from jax.experimental.pallas import tpu as pltpu
from jax.sharding import PartitionSpec as P

HD = 64
MESH = pl.DeviceIdType.MESH
TILE = 16


def dims_of(dp, fsdp):
    core = (fsdp, 2 if dp % 2 == 0 else 1)
    rest, stride = dp // core[1], fsdp * core[1]
    sizes = []
    while rest > 1:
        step = 2 if rest % 4 else 4
        if not sizes and rest % 2 == 0:
            step = 2
        if rest % step:
            step = rest
        sizes.append((stride, step))
        stride, rest = stride * step, rest // step
    return core, [(1, fsdp)] + sizes


def plan_of(dp, fsdp, rows):
    core, links = dims_of(dp, fsdp)
    tiles = rows // TILE
    if len(links) != 3 or tiles < 2:
        return [(0, rows, [core] + links)]
    y, x, z = links
    most = max(1, min(tiles - 1, (tiles * 7 + 5) // 11))
    orders = [[core, y, x, z], [core, x, z, y]]
    plan, start = [], 0
    for count, order in zip((most, tiles - most), orders):
        plan.append((start * TILE, count * TILE, order))
        start += count
    return plan


def prod_of(order):
    total = 1
    for _, size in order:
        total *= size
    return total


def coord(me, dim):
    return lax.rem(me // dim[0], dim[1])


def moved(slab, dim, old, new):
    return slab + (new - old) * dim[0]


def spread(slab, me, dims, k):
    for dim in reversed(dims):
        slab = moved(slab, dim, coord(me, dim), lax.rem(k, dim[1]))
        k = k // dim[1]
    return slab


def together(counts, visits):
    least = min(counts)
    if any(count % least for count in counts):
        for count, visit in zip(counts, visits):
            together([count], [visit])
        return

    def step(t, _):
        for count, visit in zip(counts, visits):
            times = count // least
            for u in range(times):
                visit(t * times + u)
        return 0

    lax.fori_loop(0, least, step, 0)


def whoami(fsdp):
    return lax.axis_index("dp") * fsdp + lax.axis_index("fsdp")


def place(number, fsdp):
    return (number // fsdp, lax.rem(number, fsdp))


def greet(me, dims, fsdp):
    barrier = pltpu.get_barrier_semaphore()
    count = 0
    for dim in dims:
        mine = coord(me, dim)
        for r in range(dim[1] - 1):
            peer = moved(me, dim, mine, lax.rem(mine + 1 + r, dim[1]))
            pl.semaphore_signal(barrier, inc=1, device_id=place(peer, fsdp), device_id_type=MESH)
            count += 1
    pl.semaphore_wait(barrier, count)


def gather_kernel(dp, fsdp, plan, *refs):
    *parts, out_ref, x_ref, send_sem, recv_sem, own_sem = refs
    me = whoami(fsdp)
    blocks, width = [], x_ref.shape[1]
    for ref in parts:
        for j in range(ref.shape[1] // width):
            blocks.append(ref[:, j * width : (j + 1) * width].astype(jnp.float32))
    x_ref[...] = jnp.concatenate(blocks, axis=0).astype(x_ref.dtype)
    greet(me, plan[0][2], fsdp)
    own = pltpu.make_async_copy(x_ref, out_ref.at[me], own_sem)
    own.start()

    def copy_of(band, slab, slot, peer, first):
        start, rows, _ = plan[band]
        here = out_ref.at[slab, pl.ds(start, rows), :]
        source = x_ref.at[pl.ds(start, rows), :] if first else here
        return pltpu.make_async_remote_copy(
            src_ref=source,
            dst_ref=here,
            send_sem=send_sem.at[band, slot],
            recv_sem=recv_sem.at[band, slab],
            device_id=place(peer, fsdp),
            device_id_type=MESH,
        )

    bases = []
    for _, _, order in plan:
        tree = order[:0:-1] + order[:1]
        base, at = {}, 0
        for i in range(-1, len(tree)):
            arrivals = 1 if i < 0 else prod_of(tree[:i]) * (tree[i][1] - 1)
            for j in range(i + 1, len(tree)):
                base[i, j] = at
                at += arrivals * (tree[j][1] - 1)
        bases.append(base)
    depth = len(plan[0][2])
    for i in range(-1, depth):
        counts, visits = [], []
        for band in range(len(plan)):
            order = plan[band][2]
            tree = order[:0:-1] + order[:1]

            def sends(slab, k, act, i=i, band=band, tree=tree):
                for j in range(i + 1, depth):
                    dim = tree[j]
                    mine = coord(me, dim)
                    for r in range(dim[1] - 1):
                        peer = moved(me, dim, mine, lax.rem(mine + 1 + r, dim[1]))
                        slot = bases[band][i, j] + k * (dim[1] - 1) + r
                        act(copy_of(band, slab, slot, peer, i < 0))

            if i < 0:
                sends(me, 0, lambda c: c.start())
                continue
            dim = tree[i]
            mine = coord(me, dim)

            def arrived(k, i=i, band=band, tree=tree, dim=dim, mine=mine, sends=sends):
                gap = dim[1] - 1
                peer = moved(me, dim, mine, lax.rem(mine + 1 + lax.rem(k, gap), dim[1]))
                slab = spread(peer, me, tree[:i], k // gap)
                copy_of(band, slab, 0, peer, False).wait_recv()
                sends(slab, k, lambda c: c.start())

            counts.append(prod_of(tree[:i]) * (dim[1] - 1))
            visits.append(arrived)
        if i >= 0:
            together(counts, visits)
    own.wait()
    for band in range(len(plan)):
        peer = moved(me, plan[band][2][0], coord(me, plan[band][2][0]), 1 - coord(me, plan[band][2][0]))

        def sent(slot, _, band=band, peer=peer):
            copy_of(band, me, slot, peer, True).wait_send()
            return 0

        lax.fori_loop(0, dp * fsdp - 1, sent, 0)


def gather(dp, fsdp, parts, rows, width):
    plan = plan_of(dp, fsdp, rows)
    n = dp * fsdp
    return pl.pallas_call(
        partial(gather_kernel, dp, fsdp, plan),
        out_shape=jax.ShapeDtypeStruct((n, rows, width), parts[0].dtype),
        in_specs=[pl.BlockSpec(memory_space=pltpu.VMEM)] * len(parts),
        out_specs=pl.BlockSpec(memory_space=pl.ANY),
        scratch_shapes=[
            pltpu.VMEM((rows, width), parts[0].dtype),
            pltpu.SemaphoreType.DMA((len(plan), n)),
            pltpu.SemaphoreType.DMA((len(plan), n)),
            pltpu.SemaphoreType.DMA,
        ],
        compiler_params=pltpu.CompilerParams(collective_id=0, has_side_effects=True, vmem_limit_bytes=6 * 1024 * 1024),
        name="gather_params",
    )(*parts)


def sum_kernel(dp, fsdp, plan, x_ref, out_ref, *scratch):
    bands = len(plan)
    kept, held = scratch[:bands], scratch[bands : 2 * bands]
    send_sem, recv_sem, own_sem = scratch[2 * bands :]
    me = whoami(fsdp)
    greet(me, plan[0][2], fsdp)
    f32 = jnp.float32
    depth = len(plan[0][2])
    bases = []
    for _, _, order in plan:
        base, at = [], 0
        for i in range(depth):
            base.append(at)
            at += prod_of(order[i + 1 :]) * (order[i][1] - 1)
        bases.append(base)

    def sending(band, i, source, r, rest):
        dim = plan[band][2][i]
        mine = coord(me, dim)
        gap = dim[1] - 1
        there = lax.rem(mine + 1 + r, dim[1])
        back = lax.rem(mine - there - 1 + 2 * dim[1], dim[1])
        slot = bases[band][i] + rest * gap + back
        return pltpu.make_async_remote_copy(
            src_ref=source,
            dst_ref=held[band].at[slot],
            send_sem=send_sem.at[band, bases[band][i] + rest * gap + r],
            recv_sem=recv_sem.at[band, slot],
            device_id=place(moved(me, dim, mine, there), fsdp),
            device_id_type=MESH,
        )

    def own_copy(band, index):
        start, rows, order = plan[band]
        slab = spread(me, me, order[1:], index)
        return pltpu.make_async_copy(
            x_ref.at[slab, pl.ds(start, rows), :], kept[band].at[index], own_sem.at[band, index]
        )

    def step_of(band, i, t):
        order = plan[band][2]
        if i == depth - 1:
            return 0, 0, 0
        dim = order[i + 1]
        inner = prod_of(order[i + 2 :])
        r, rest = t // inner, lax.rem(t, inner)
        return r, rest, lax.rem(coord(me, dim) + 1 + r, dim[1]) * inner + rest

    counts, visits = [], []
    for band in range(bands):
        start, rows, order = plan[band]
        core = order[0]
        mine = coord(me, core)

        def begin(t, band=band, start=start, rows=rows, order=order, core=core, mine=mine):
            index = step_of(band, 0, t)[2]
            slab = moved(spread(me, me, order[1:], index), core, mine, lax.rem(mine + 1, core[1]))
            sending(band, 0, x_ref.at[slab, pl.ds(start, rows), :], 0, index).start()
            own_copy(band, index).start()

        counts.append(prod_of(order[1:]))
        visits.append(begin)
    together(counts, visits)
    for i in range(depth):
        counts, visits = [], []
        for band in range(bands):
            start, rows, order = plan[band]
            gap = order[i][1] - 1
            where = 0
            for dim in order[1 : i + 1]:
                where = where * dim[1] + coord(me, dim)
            where = where * prod_of(order[i + 1 :])

            def visit(t, i=i, band=band, start=start, rows=rows, order=order, gap=gap, where=where):
                r, rest, index = step_of(band, i, t)
                if i == 0:
                    own_copy(band, index).wait()
                total = kept[band][where + index].astype(f32)
                for q in range(gap):
                    slot = bases[band][i] + index * gap + q
                    pltpu.make_async_remote_copy(
                        src_ref=held[band].at[slot],
                        dst_ref=held[band].at[slot],
                        send_sem=send_sem.at[band, 0],
                        recv_sem=recv_sem.at[band, slot],
                        device_id=place(moved(me, order[0], coord(me, order[0]), 1 - coord(me, order[0])), fsdp),
                        device_id_type=MESH,
                    ).wait_recv()
                    total = total + held[band][slot].astype(f32)
                if i == depth - 1:
                    out_ref[start : start + rows, :] = total
                    return
                kept[band][where + index] = total.astype(kept[band].dtype)

                @pl.when(r < order[i + 1][1] - 1)
                def _():
                    sending(band, i + 1, kept[band].at[where + index], r, rest).start()

            counts.append(prod_of(order[i + 1 :]))
            visits.append(visit)
        together(counts, visits)
    for band in range(bands):
        start, rows, order = plan[band]

        def sent(slot, _, band=band):
            core = plan[band][2][0]
            pltpu.make_async_remote_copy(
                src_ref=held[band].at[0],
                dst_ref=held[band].at[0],
                send_sem=send_sem.at[band, slot],
                recv_sem=recv_sem.at[band, 0],
                device_id=place(moved(me, core, coord(me, core), 1 - coord(me, core)), fsdp),
                device_id_type=MESH,
            ).wait_send()
            return 0

        lax.fori_loop(0, dp * fsdp - 1, sent, 0)


def sum_shards(dp, fsdp, terms):
    n, rows, width = terms.shape
    plan = plan_of(dp, fsdp, rows)
    return pl.pallas_call(
        partial(sum_kernel, dp, fsdp, plan),
        out_shape=jax.ShapeDtypeStruct((rows, width), jnp.float32),
        in_specs=[pl.BlockSpec(memory_space=pl.ANY)],
        out_specs=pl.BlockSpec(memory_space=pltpu.VMEM),
        scratch_shapes=[pltpu.VMEM((n // 2, band[1], width), terms.dtype) for band in plan]
        + [pltpu.VMEM((n - 1, band[1], width), terms.dtype) for band in plan]
        + [
            pltpu.SemaphoreType.DMA((len(plan), n)),
            pltpu.SemaphoreType.DMA((len(plan), n)),
            pltpu.SemaphoreType.DMA((len(plan), n // 2)),
        ],
        compiler_params=pltpu.CompilerParams(
            collective_id=1, has_side_effects=True, vmem_limit_bytes=28 * 1024 * 1024 if n <= 64 else 56 * 1024 * 1024
        ),
        name="sum_grads",
    )(terms)


PARAM_NAMES = [
    "query_weight",
    "key_weight",
    "value_weight",
    "query_bias",
    "value_bias",
    "out_weight",
    "out_bias",
    "first_gain",
    "first_shift",
    "up_weight",
    "up_bias",
    "down_weight",
    "down_bias",
    "second_gain",
    "second_shift",
]
VECTORS = [name for name in PARAM_NAMES if not name.endswith("_weight")]

def normalize(rows, gain, shift):
    centred = rows - jnp.mean(rows, axis=-1, keepdims=True)
    scale = lax.rsqrt(jnp.mean(centred * centred, axis=-1, keepdims=True) + 1e-06)
    normed = centred * scale
    return (normed * gain + shift, normed, scale)


def norm_back(grad, normed, scale, gain):
    scaled = grad * gain
    return scale * (
        scaled
        - jnp.mean(scaled, axis=-1, keepdims=True)
        - normed * jnp.mean(scaled * normed, axis=-1, keepdims=True)
    )


def rowdot(left, right):
    return jnp.einsum("ti,to->io", left, right, preferred_element_type=jnp.float32)


def backdot(left, right):
    return jnp.einsum("to,io->ti", left, right, preferred_element_type=jnp.float32)


def on_device(
    dp,
    fsdp,
    tokens,
    query_weight,
    key_weight,
    value_weight,
    query_bias,
    value_bias,
    out_weight,
    out_bias,
    first_gain,
    first_shift,
    up_weight,
    up_bias,
    down_weight,
    down_bias,
    second_gain,
    second_shift,
    segment_ids,
    out_grad,
):
    bf16 = jnp.bfloat16
    width = tokens.shape[1]
    n = dp * fsdp
    given = dict(
        query_bias=query_bias,
        value_bias=value_bias,
        out_bias=out_bias,
        first_gain=first_gain,
        first_shift=first_shift,
        up_bias=up_bias,
        down_bias=down_bias,
        second_gain=second_gain,
        second_shift=second_shift,
    )
    part = query_weight.shape[0]
    wide = up_weight.shape[1] // width
    tall = down_weight.shape[0]
    used = (4 + wide) * part + tall
    lines = len(VECTORS)
    total_rows = -(-(used + lines) // TILE) * TILE
    row = lax.broadcasted_iota(jnp.int32, (total_rows - used, width), 0)
    flat = jnp.zeros((total_rows - used, width), jnp.float32)
    for k, name in enumerate(VECTORS):
        padded = jnp.pad(given[name].astype(jnp.float32), (0, width - given[name].shape[0]))
        flat = jnp.where(row == k, padded[None, :], flat)
    flat = flat.astype(bf16)
    parts = [query_weight, key_weight, value_weight, out_weight, up_weight, down_weight, flat]
    if part % 8 or tall % 8:
        wides = [up_weight[:, j * width : (j + 1) * width] for j in range(wide)]
        parts = [jnp.concatenate(parts[:4] + wides + parts[5:], axis=0)]
    slabs = gather(dp, fsdp, parts, total_rows, width)

    def matrix(k):
        return slabs[:, k * part : (k + 1) * part, :].reshape(n * part, width)

    params = dict(
        query_weight=matrix(0),
        key_weight=matrix(1),
        value_weight=matrix(2),
        out_weight=matrix(3),
        up_weight=jnp.concatenate([matrix(4 + j) for j in range(wide)], axis=1),
        down_weight=slabs[:, (4 + wide) * part : used, :].reshape(n * tall, width),
    )
    for k, name in enumerate(VECTORS):
        params[name] = slabs[:, used + k, : given[name].shape[0]].reshape(-1)
    length = tokens.shape[0]
    width = tokens.shape[1]
    heads = width // HD
    f32 = jnp.float32
    bf16 = jnp.bfloat16

    def split_heads(rows):
        return rows.reshape(length, heads, HD)

    query = (
        jnp.dot(tokens, params["query_weight"], preferred_element_type=f32)
        + params["query_bias"].astype(f32)
    ).astype(bf16)
    keys = jnp.dot(tokens, params["key_weight"], preferred_element_type=f32).astype(bf16)
    values = (
        jnp.dot(tokens, params["value_weight"], preferred_element_type=f32)
        + params["value_bias"].astype(f32)
    ).astype(bf16)
    same = (segment_ids[0][:, None] == segment_ids[0][None, :])[None]
    scores = (
        jnp.einsum(
            "qhd,khd->hqk", split_heads(query), split_heads(keys), preferred_element_type=f32
        )
        * 0.125
    )
    masked = jnp.where(same, scores, -1e30)
    top = jnp.max(masked, axis=-1, keepdims=True)
    expo = jnp.exp(masked - top)
    total = jnp.sum(expo, axis=-1, keepdims=True)
    probs = expo / total
    probs_low = probs.astype(bf16)
    attended = (
        jnp.einsum("hqk,khd->qhd", probs_low, split_heads(values), preferred_element_type=f32)
        .reshape(length, width)
        .astype(bf16)
    )
    branch = jnp.dot(attended, params["out_weight"], preferred_element_type=f32) + params[
        "out_bias"
    ].astype(f32)
    gain_first = params["first_gain"].astype(f32)
    first, normed_first, scale_first = normalize(
        tokens.astype(f32) + branch, gain_first, params["first_shift"].astype(f32)
    )
    first_low = first.astype(bf16)
    hidden = jnp.dot(first_low, params["up_weight"], preferred_element_type=f32) + params[
        "up_bias"
    ].astype(f32)
    active_full, gelu_back = jax.vjp(partial(jax.nn.gelu, approximate=False), hidden)
    active = active_full.astype(bf16)
    second_in = (
        first
        + jnp.dot(active, params["down_weight"], preferred_element_type=f32)
        + params["down_bias"].astype(f32)
    )
    gain_second = params["second_gain"].astype(f32)
    result, normed_second, scale_second = normalize(
        second_in, gain_second, params["second_shift"].astype(f32)
    )
    layer_output = result.astype(bf16)
    grad_out = out_grad.astype(f32)
    grads = {}
    grads["second_gain"] = jnp.sum(grad_out * normed_second, axis=0)
    grads["second_shift"] = jnp.sum(grad_out, axis=0)
    d_second = norm_back(grad_out, normed_second, scale_second, gain_second)
    d_down = d_second.astype(bf16)
    grads["down_bias"] = jnp.sum(d_down.astype(f32), axis=0)
    grads["down_weight"] = rowdot(active, d_down)
    d_hidden = gelu_back(backdot(d_down, params["down_weight"]))[0].astype(bf16)
    grads["up_bias"] = jnp.sum(d_hidden.astype(f32), axis=0)
    grads["up_weight"] = rowdot(first_low, d_hidden)
    d_first = d_second + backdot(d_hidden, params["up_weight"])
    grads["first_gain"] = jnp.sum(d_first * normed_first, axis=0)
    grads["first_shift"] = jnp.sum(d_first, axis=0)
    d_branch_full = norm_back(d_first, normed_first, scale_first, gain_first)
    d_branch = d_branch_full.astype(bf16)
    grads["out_bias"] = jnp.sum(d_branch.astype(f32), axis=0)
    grads["out_weight"] = rowdot(attended, d_branch)
    d_attended = split_heads(backdot(d_branch, params["out_weight"]).astype(bf16))
    d_probs = jnp.einsum(
        "qhd,khd->hqk", d_attended, split_heads(values), preferred_element_type=f32
    )
    d_scores = (probs * (d_probs - jnp.sum(d_probs * probs, axis=-1, keepdims=True))).astype(bf16)
    d_query = (
        (
            jnp.einsum("hqk,khd->qhd", d_scores, split_heads(keys), preferred_element_type=f32)
            * 0.125
        )
        .reshape(length, width)
        .astype(bf16)
    )
    d_keys = (
        (
            jnp.einsum("hqk,qhd->khd", d_scores, split_heads(query), preferred_element_type=f32)
            * 0.125
        )
        .reshape(length, width)
        .astype(bf16)
    )
    d_values = (
        jnp.einsum("hqk,qhd->khd", probs_low, d_attended, preferred_element_type=f32)
        .reshape(length, width)
        .astype(bf16)
    )
    grads["query_weight"] = rowdot(tokens, d_query)
    grads["key_weight"] = rowdot(tokens, d_keys)
    grads["value_weight"] = rowdot(tokens, d_values)
    grads["query_bias"] = jnp.sum(d_query.astype(f32), axis=0)
    grads["value_bias"] = jnp.sum(d_values.astype(f32), axis=0)
    input_grad = (
        d_branch_full
        + backdot(d_query, params["query_weight"])
        + backdot(d_keys, params["key_weight"])
        + backdot(d_values, params["value_weight"])
    )
    def by_owner(value):
        return value.astype(bf16).reshape(n, -1, width)

    row = lax.broadcasted_iota(jnp.int32, (n, total_rows - used, width), 1)
    flat = jnp.zeros((n, total_rows - used, width), f32)
    for k, name in enumerate(VECTORS):
        mine = grads[name].reshape(n, -1)
        mine = jnp.pad(mine, ((0, 0), (0, width - mine.shape[1])))
        flat = jnp.where(row == k, mine[:, None, :], flat)
    flat = flat.astype(bf16)
    up = grads["up_weight"].astype(bf16)
    terms = jnp.concatenate(
        [by_owner(grads[name + "_weight"]) for name in ("query", "key", "value", "out")]
        + [by_owner(up[:, j * width : (j + 1) * width]) for j in range(wide)]
        + [by_owner(grads["down_weight"]), flat],
        axis=1,
    )
    sums = sum_shards(dp, fsdp, terms)
    owned = {}
    for k, name in enumerate(("query", "key", "value", "out")):
        owned[name + "_weight"] = sums[k * part : (k + 1) * part]
    owned["up_weight"] = jnp.concatenate(
        [sums[(4 + j) * part : (5 + j) * part] for j in range(wide)], axis=1
    )
    owned["down_weight"] = sums[(4 + wide) * part : used]
    for k, name in enumerate(VECTORS):
        owned[name] = sums[used + k, : given[name].shape[0]]
    return tuple([layer_output, input_grad] + [owned[name] for name in PARAM_NAMES])


def solution(mesh):
    in_specs = (
        P(("dp", "fsdp"), None),
        P(("dp", "fsdp"), None),
        P(("dp", "fsdp"), None),
        P(("dp", "fsdp"), None),
        P(("dp", "fsdp")),
        P(("dp", "fsdp")),
        P(("dp", "fsdp"), None),
        P(("dp", "fsdp")),
        P(("dp", "fsdp")),
        P(("dp", "fsdp")),
        P(("dp", "fsdp"), None),
        P(("dp", "fsdp")),
        P(("dp", "fsdp"), None),
        P(("dp", "fsdp")),
        P(("dp", "fsdp")),
        P(("dp", "fsdp")),
        P(("dp", "fsdp"), None),
        P(("dp", "fsdp"), None),
    )
    out_specs = (
        P(("dp", "fsdp"), None),
        P(("dp", "fsdp"), None),
        P(("dp", "fsdp"), None),
        P(("dp", "fsdp"), None),
        P(("dp", "fsdp"), None),
        P(("dp", "fsdp")),
        P(("dp", "fsdp")),
        P(("dp", "fsdp"), None),
        P(("dp", "fsdp")),
        P(("dp", "fsdp")),
        P(("dp", "fsdp")),
        P(("dp", "fsdp"), None),
        P(("dp", "fsdp")),
        P(("dp", "fsdp"), None),
        P(("dp", "fsdp")),
        P(("dp", "fsdp")),
        P(("dp", "fsdp")),
    )
    return jax.shard_map(
        partial(on_device, mesh.shape["dp"], mesh.shape["fsdp"]),
        mesh=mesh,
        in_specs=in_specs,
        out_specs=out_specs,
        check_vma=False,
    )
```

```python
import math
from functools import partial

import jax
import jax.numpy as jnp
from jax import lax
from jax.experimental import pallas as pl
from jax.experimental.pallas import tpu as pltpu
from jax.sharding import PartitionSpec as P

HD = 64
MESH = pl.DeviceIdType.MESH
TILE = 16


def dims_of(dp, fsdp):
    core = (fsdp, 2 if dp % 2 == 0 else 1)
    rest, stride = dp // core[1], fsdp * core[1]
    sizes = []
    while rest > 1:
        step = 2 if rest % 4 else 4
        if not sizes and rest % 2 == 0:
            step = 2
        if rest % step:
            step = rest
        sizes.append((stride, step))
        stride, rest = stride * step, rest // step
    return core, [(1, fsdp)] + sizes


def plan_of(dp, fsdp, rows):
    core, links = dims_of(dp, fsdp)
    tiles = rows // TILE
    if len(links) != 3 or tiles < 2:
        return [(0, rows, [core] + links)]
    y, x, z = links
    most = max(1, min(tiles - 1, (tiles * 7 + 5) // 11))
    orders = [[core, y, x, z], [core, x, z, y]]
    plan, start = [], 0
    for count, order in zip((most, tiles - most), orders):
        plan.append((start * TILE, count * TILE, order))
        start += count
    return plan


def prod_of(order):
    total = 1
    for _, size in order:
        total *= size
    return total


def coord(me, dim):
    return lax.rem(me // dim[0], dim[1])


def moved(slab, dim, old, new):
    return slab + (new - old) * dim[0]


def spread(slab, me, dims, k):
    for dim in reversed(dims):
        slab = moved(slab, dim, coord(me, dim), lax.rem(k, dim[1]))
        k = k // dim[1]
    return slab


def together(counts, visits):
    least = min(counts)
    if any(count % least for count in counts):
        for count, visit in zip(counts, visits):
            together([count], [visit])
        return

    def step(t, _):
        for count, visit in zip(counts, visits):
            times = count // least
            for u in range(times):
                visit(t * times + u)
        return 0

    lax.fori_loop(0, least, step, 0)


def whoami(fsdp):
    return lax.axis_index("dp") * fsdp + lax.axis_index("fsdp")


def place(number, fsdp):
    return (number // fsdp, lax.rem(number, fsdp))


def greet(me, dims, fsdp):
    barrier = pltpu.get_barrier_semaphore()
    count = 0
    for dim in dims:
        mine = coord(me, dim)
        for r in range(dim[1] - 1):
            peer = moved(me, dim, mine, lax.rem(mine + 1 + r, dim[1]))
            pl.semaphore_signal(barrier, inc=1, device_id=place(peer, fsdp), device_id_type=MESH)
            count += 1
    pl.semaphore_wait(barrier, count)


def gather_kernel(dp, fsdp, plan, *refs):
    *parts, out_ref, x_ref, send_sem, recv_sem, own_sem = refs
    me = whoami(fsdp)
    blocks, width = [], x_ref.shape[1]
    for ref in parts:
        for j in range(ref.shape[1] // width):
            blocks.append(ref[:, j * width : (j + 1) * width].astype(jnp.float32))
    x_ref[...] = jnp.concatenate(blocks, axis=0).astype(x_ref.dtype)
    greet(me, plan[0][2], fsdp)
    own = pltpu.make_async_copy(x_ref, out_ref.at[me], own_sem)
    own.start()

    def copy_of(band, slab, slot, peer, first):
        start, rows, _ = plan[band]
        here = out_ref.at[slab, pl.ds(start, rows), :]
        source = x_ref.at[pl.ds(start, rows), :] if first else here
        return pltpu.make_async_remote_copy(
            src_ref=source,
            dst_ref=here,
            send_sem=send_sem.at[band, slot],
            recv_sem=recv_sem.at[band, slab],
            device_id=place(peer, fsdp),
            device_id_type=MESH,
        )

    bases = []
    for _, _, order in plan:
        tree = order[:0:-1] + order[:1]
        base, at = {}, 0
        for i in range(-1, len(tree)):
            arrivals = 1 if i < 0 else prod_of(tree[:i]) * (tree[i][1] - 1)
            for j in range(i + 1, len(tree)):
                base[i, j] = at
                at += arrivals * (tree[j][1] - 1)
        bases.append(base)
    depth = len(plan[0][2])
    for i in range(-1, depth):
        counts, visits = [], []
        for band in range(len(plan)):
            order = plan[band][2]
            tree = order[:0:-1] + order[:1]

            def sends(slab, k, act, i=i, band=band, tree=tree):
                for j in range(i + 1, depth):
                    dim = tree[j]
                    mine = coord(me, dim)
                    for r in range(dim[1] - 1):
                        peer = moved(me, dim, mine, lax.rem(mine + 1 + r, dim[1]))
                        slot = bases[band][i, j] + k * (dim[1] - 1) + r
                        act(copy_of(band, slab, slot, peer, i < 0))

            if i < 0:
                sends(me, 0, lambda c: c.start())
                continue
            dim = tree[i]
            mine = coord(me, dim)

            def arrived(k, i=i, band=band, tree=tree, dim=dim, mine=mine, sends=sends):
                gap = dim[1] - 1
                peer = moved(me, dim, mine, lax.rem(mine + 1 + lax.rem(k, gap), dim[1]))
                slab = spread(peer, me, tree[:i], k // gap)
                copy_of(band, slab, 0, peer, False).wait_recv()
                sends(slab, k, lambda c: c.start())

            counts.append(prod_of(tree[:i]) * (dim[1] - 1))
            visits.append(arrived)
        if i >= 0:
            together(counts, visits)
    own.wait()
    for band in range(len(plan)):
        peer = moved(me, plan[band][2][0], coord(me, plan[band][2][0]), 1 - coord(me, plan[band][2][0]))

        def sent(slot, _, band=band, peer=peer):
            copy_of(band, me, slot, peer, True).wait_send()
            return 0

        lax.fori_loop(0, dp * fsdp - 1, sent, 0)


def gather(dp, fsdp, parts, rows, width):
    plan = plan_of(dp, fsdp, rows)
    n = dp * fsdp
    return pl.pallas_call(
        partial(gather_kernel, dp, fsdp, plan),
        out_shape=jax.ShapeDtypeStruct((n, rows, width), parts[0].dtype),
        in_specs=[pl.BlockSpec(memory_space=pltpu.VMEM)] * len(parts),
        out_specs=pl.BlockSpec(memory_space=pl.ANY),
        scratch_shapes=[
            pltpu.VMEM((rows, width), parts[0].dtype),
            pltpu.SemaphoreType.DMA((len(plan), n)),
            pltpu.SemaphoreType.DMA((len(plan), n)),
            pltpu.SemaphoreType.DMA,
        ],
        compiler_params=pltpu.CompilerParams(collective_id=0, has_side_effects=True, vmem_limit_bytes=6 * 1024 * 1024),
        name="gather_params",
    )(*parts)


def sum_kernel(dp, fsdp, plan, x_ref, out_ref, *scratch):
    bands = len(plan)
    kept, held = scratch[:bands], scratch[bands : 2 * bands]
    send_sem, recv_sem, own_sem = scratch[2 * bands :]
    me = whoami(fsdp)
    greet(me, plan[0][2], fsdp)
    f32 = jnp.float32
    depth = len(plan[0][2])
    bases = []
    for _, _, order in plan:
        base, at = [], 0
        for i in range(depth):
            base.append(at)
            at += prod_of(order[i + 1 :]) * (order[i][1] - 1)
        bases.append(base)

    def sending(band, i, source, r, rest):
        dim = plan[band][2][i]
        mine = coord(me, dim)
        gap = dim[1] - 1
        there = lax.rem(mine + 1 + r, dim[1])
        back = lax.rem(mine - there - 1 + 2 * dim[1], dim[1])
        slot = bases[band][i] + rest * gap + back
        return pltpu.make_async_remote_copy(
            src_ref=source,
            dst_ref=held[band].at[slot],
            send_sem=send_sem.at[band, bases[band][i] + rest * gap + r],
            recv_sem=recv_sem.at[band, slot],
            device_id=place(moved(me, dim, mine, there), fsdp),
            device_id_type=MESH,
        )

    def own_copy(band, index):
        start, rows, order = plan[band]
        slab = spread(me, me, order[1:], index)
        return pltpu.make_async_copy(
            x_ref.at[slab, pl.ds(start, rows), :], kept[band].at[index], own_sem.at[band, index]
        )

    def step_of(band, i, t):
        order = plan[band][2]
        if i == depth - 1:
            return 0, 0, 0
        dim = order[i + 1]
        inner = prod_of(order[i + 2 :])
        r, rest = t // inner, lax.rem(t, inner)
        return r, rest, lax.rem(coord(me, dim) + 1 + r, dim[1]) * inner + rest

    counts, visits = [], []
    for band in range(bands):
        start, rows, order = plan[band]
        core = order[0]
        mine = coord(me, core)

        def begin(t, band=band, start=start, rows=rows, order=order, core=core, mine=mine):
            index = step_of(band, 0, t)[2]
            slab = moved(spread(me, me, order[1:], index), core, mine, lax.rem(mine + 1, core[1]))
            sending(band, 0, x_ref.at[slab, pl.ds(start, rows), :], 0, index).start()
            own_copy(band, index).start()

        counts.append(prod_of(order[1:]))
        visits.append(begin)
    together(counts, visits)
    for i in range(depth):
        counts, visits = [], []
        for band in range(bands):
            start, rows, order = plan[band]
            gap = order[i][1] - 1
            where = 0
            for dim in order[1 : i + 1]:
                where = where * dim[1] + coord(me, dim)
            where = where * prod_of(order[i + 1 :])

            def visit(t, i=i, band=band, start=start, rows=rows, order=order, gap=gap, where=where):
                r, rest, index = step_of(band, i, t)
                if i == 0:
                    own_copy(band, index).wait()
                total = kept[band][where + index].astype(f32)
                for q in range(gap):
                    slot = bases[band][i] + index * gap + q
                    pltpu.make_async_remote_copy(
                        src_ref=held[band].at[slot],
                        dst_ref=held[band].at[slot],
                        send_sem=send_sem.at[band, 0],
                        recv_sem=recv_sem.at[band, slot],
                        device_id=place(moved(me, order[0], coord(me, order[0]), 1 - coord(me, order[0])), fsdp),
                        device_id_type=MESH,
                    ).wait_recv()
                    total = total + held[band][slot].astype(f32)
                if i == depth - 1:
                    out_ref[start : start + rows, :] = total
                    return
                kept[band][where + index] = total.astype(kept[band].dtype)

                @pl.when(r < order[i + 1][1] - 1)
                def _():
                    sending(band, i + 1, kept[band].at[where + index], r, rest).start()

            counts.append(prod_of(order[i + 1 :]))
            visits.append(visit)
        together(counts, visits)
    for band in range(bands):
        start, rows, order = plan[band]

        def sent(slot, _, band=band):
            core = plan[band][2][0]
            pltpu.make_async_remote_copy(
                src_ref=held[band].at[0],
                dst_ref=held[band].at[0],
                send_sem=send_sem.at[band, slot],
                recv_sem=recv_sem.at[band, 0],
                device_id=place(moved(me, core, coord(me, core), 1 - coord(me, core)), fsdp),
                device_id_type=MESH,
            ).wait_send()
            return 0

        lax.fori_loop(0, dp * fsdp - 1, sent, 0)


def sum_shards(dp, fsdp, terms):
    n, rows, width = terms.shape
    plan = plan_of(dp, fsdp, rows)
    return pl.pallas_call(
        partial(sum_kernel, dp, fsdp, plan),
        out_shape=jax.ShapeDtypeStruct((rows, width), jnp.float32),
        in_specs=[pl.BlockSpec(memory_space=pl.ANY)],
        out_specs=pl.BlockSpec(memory_space=pltpu.VMEM),
        scratch_shapes=[pltpu.VMEM((n // 2, band[1], width), terms.dtype) for band in plan]
        + [pltpu.VMEM((n - 1, band[1], width), terms.dtype) for band in plan]
        + [
            pltpu.SemaphoreType.DMA((len(plan), n)),
            pltpu.SemaphoreType.DMA((len(plan), n)),
            pltpu.SemaphoreType.DMA((len(plan), n // 2)),
        ],
        compiler_params=pltpu.CompilerParams(
            collective_id=1, has_side_effects=True, vmem_limit_bytes=28 * 1024 * 1024 if n <= 64 else 56 * 1024 * 1024
        ),
        name="sum_grads",
    )(terms)


PARAM_NAMES = [
    "query_weight",
    "key_weight",
    "value_weight",
    "query_bias",
    "value_bias",
    "out_weight",
    "out_bias",
    "first_gain",
    "first_shift",
    "up_weight",
    "up_bias",
    "down_weight",
    "down_bias",
    "second_gain",
    "second_shift",
]
VECTORS = [name for name in PARAM_NAMES if not name.endswith("_weight")]

def terms_kernel(part, tall, *refs):
    tokens, d_query, d_keys, d_values, attended, d_branch, first_low, d_hidden, active, d_down, flat, out_ref = refs
    width = out_ref.shape[2]

    def product(left, right, start, count, rows):
        whole = lax.dot_general(
            left[:, start : start + count], right, (((0,), (0,)), ((), ())), preferred_element_type=jnp.float32
        )
        return whole.reshape(count // rows, rows, width)

    pairs = [(tokens, d_query[...]), (tokens, d_keys[...]), (tokens, d_values[...]), (attended, d_branch[...])]
    for j in range(d_hidden.shape[1] // width):
        pairs.append((first_low, d_hidden[:, j * width : (j + 1) * width]))
    count = math.lcm(part, 128)
    for start in range(0, width, count):
        slabs = slice(start // part, (start + count) // part)
        for k in range(0, len(pairs), 2):
            two = [product(left, right, start, count, part) for left, right in pairs[k : k + 2]]
            out_ref[slabs, k * part : (k + 2) * part, :] = jnp.concatenate(two, axis=1).astype(out_ref.dtype)
    count, at = math.lcm(tall, 128), len(pairs) * part
    for start in range(0, active.shape[1], count):
        slabs = slice(start // tall, (start + count) // tall)
        out_ref[slabs, at : at + tall, :] = product(active, d_down[...], start, count, tall).astype(out_ref.dtype)
    out_ref[:, at + tall :, :] = flat[...]


def terms_by_owner(part, tall, rows, operands):
    n, _, width = operands[-1].shape
    return pl.pallas_call(
        partial(terms_kernel, part, tall),
        out_shape=jax.ShapeDtypeStruct((n, rows, width), jnp.bfloat16),
        in_specs=[pl.BlockSpec(memory_space=pltpu.VMEM)] * len(operands),
        out_specs=pl.BlockSpec(memory_space=pltpu.VMEM),
        compiler_params=pltpu.CompilerParams(vmem_limit_bytes=32 * 1024 * 1024),
        name="terms_by_owner",
    )(*operands)


def normalize(rows, gain, shift):
    centred = rows - jnp.mean(rows, axis=-1, keepdims=True)
    scale = lax.rsqrt(jnp.mean(centred * centred, axis=-1, keepdims=True) + 1e-06)
    normed = centred * scale
    return (normed * gain + shift, normed, scale)


def norm_back(grad, normed, scale, gain):
    scaled = grad * gain
    return scale * (
        scaled
        - jnp.mean(scaled, axis=-1, keepdims=True)
        - normed * jnp.mean(scaled * normed, axis=-1, keepdims=True)
    )


def rowdot(left, right):
    return jnp.einsum("ti,to->io", left, right, preferred_element_type=jnp.float32)


def backdot(left, right):
    return jnp.einsum("to,io->ti", left, right, preferred_element_type=jnp.float32)


def on_device(
    dp,
    fsdp,
    tokens,
    query_weight,
    key_weight,
    value_weight,
    query_bias,
    value_bias,
    out_weight,
    out_bias,
    first_gain,
    first_shift,
    up_weight,
    up_bias,
    down_weight,
    down_bias,
    second_gain,
    second_shift,
    segment_ids,
    out_grad,
):
    bf16 = jnp.bfloat16
    width = tokens.shape[1]
    n = dp * fsdp
    given = dict(
        query_bias=query_bias,
        value_bias=value_bias,
        out_bias=out_bias,
        first_gain=first_gain,
        first_shift=first_shift,
        up_bias=up_bias,
        down_bias=down_bias,
        second_gain=second_gain,
        second_shift=second_shift,
    )
    part = query_weight.shape[0]
    wide = up_weight.shape[1] // width
    tall = down_weight.shape[0]
    used = (4 + wide) * part + tall
    lines = len(VECTORS)
    total_rows = -(-(used + lines) // TILE) * TILE
    row = lax.broadcasted_iota(jnp.int32, (total_rows - used, width), 0)
    flat = jnp.zeros((total_rows - used, width), jnp.float32)
    for k, name in enumerate(VECTORS):
        padded = jnp.pad(given[name].astype(jnp.float32), (0, width - given[name].shape[0]))
        flat = jnp.where(row == k, padded[None, :], flat)
    flat = flat.astype(bf16)
    parts = [query_weight, key_weight, value_weight, out_weight, up_weight, down_weight, flat]
    if part % 8 or tall % 8:
        wides = [up_weight[:, j * width : (j + 1) * width] for j in range(wide)]
        parts = [jnp.concatenate(parts[:4] + wides + parts[5:], axis=0)]
    slabs = gather(dp, fsdp, parts, total_rows, width)

    def matrix(k):
        return slabs[:, k * part : (k + 1) * part, :].reshape(n * part, width)

    params = dict(
        query_weight=matrix(0),
        key_weight=matrix(1),
        value_weight=matrix(2),
        out_weight=matrix(3),
        up_weight=jnp.concatenate([matrix(4 + j) for j in range(wide)], axis=1),
        down_weight=slabs[:, (4 + wide) * part : used, :].reshape(n * tall, width),
    )
    for k, name in enumerate(VECTORS):
        params[name] = slabs[:, used + k, : given[name].shape[0]].reshape(-1)
    length = tokens.shape[0]
    width = tokens.shape[1]
    heads = width // HD
    f32 = jnp.float32
    bf16 = jnp.bfloat16

    def split_heads(rows):
        return rows.reshape(length, heads, HD)

    query = (
        jnp.dot(tokens, params["query_weight"], preferred_element_type=f32)
        + params["query_bias"].astype(f32)
    ).astype(bf16)
    keys = jnp.dot(tokens, params["key_weight"], preferred_element_type=f32).astype(bf16)
    values = (
        jnp.dot(tokens, params["value_weight"], preferred_element_type=f32)
        + params["value_bias"].astype(f32)
    ).astype(bf16)
    same = (segment_ids[0][:, None] == segment_ids[0][None, :])[None]
    scores = (
        jnp.einsum(
            "qhd,khd->hqk", split_heads(query), split_heads(keys), preferred_element_type=f32
        )
        * 0.125
    )
    masked = jnp.where(same, scores, -1e30)
    top = jnp.max(masked, axis=-1, keepdims=True)
    expo = jnp.exp(masked - top)
    total = jnp.sum(expo, axis=-1, keepdims=True)
    probs = expo / total
    probs_low = probs.astype(bf16)
    attended = (
        jnp.einsum("hqk,khd->qhd", probs_low, split_heads(values), preferred_element_type=f32)
        .reshape(length, width)
        .astype(bf16)
    )
    branch = jnp.dot(attended, params["out_weight"], preferred_element_type=f32) + params[
        "out_bias"
    ].astype(f32)
    gain_first = params["first_gain"].astype(f32)
    first, normed_first, scale_first = normalize(
        tokens.astype(f32) + branch, gain_first, params["first_shift"].astype(f32)
    )
    first_low = first.astype(bf16)
    hidden = jnp.dot(first_low, params["up_weight"], preferred_element_type=f32) + params[
        "up_bias"
    ].astype(f32)
    active_full, gelu_back = jax.vjp(partial(jax.nn.gelu, approximate=False), hidden)
    active = active_full.astype(bf16)
    second_in = (
        first
        + jnp.dot(active, params["down_weight"], preferred_element_type=f32)
        + params["down_bias"].astype(f32)
    )
    gain_second = params["second_gain"].astype(f32)
    result, normed_second, scale_second = normalize(
        second_in, gain_second, params["second_shift"].astype(f32)
    )
    layer_output = result.astype(bf16)
    grad_out = out_grad.astype(f32)
    grads = {}
    grads["second_gain"] = jnp.sum(grad_out * normed_second, axis=0)
    grads["second_shift"] = jnp.sum(grad_out, axis=0)
    d_second = norm_back(grad_out, normed_second, scale_second, gain_second)
    d_down = d_second.astype(bf16)
    grads["down_bias"] = jnp.sum(d_down.astype(f32), axis=0)
    d_hidden = gelu_back(backdot(d_down, params["down_weight"]))[0].astype(bf16)
    grads["up_bias"] = jnp.sum(d_hidden.astype(f32), axis=0)
    d_first = d_second + backdot(d_hidden, params["up_weight"])
    grads["first_gain"] = jnp.sum(d_first * normed_first, axis=0)
    grads["first_shift"] = jnp.sum(d_first, axis=0)
    d_branch_full = norm_back(d_first, normed_first, scale_first, gain_first)
    d_branch = d_branch_full.astype(bf16)
    grads["out_bias"] = jnp.sum(d_branch.astype(f32), axis=0)
    d_attended = split_heads(backdot(d_branch, params["out_weight"]).astype(bf16))
    d_probs = jnp.einsum(
        "qhd,khd->hqk", d_attended, split_heads(values), preferred_element_type=f32
    )
    d_scores = (probs * (d_probs - jnp.sum(d_probs * probs, axis=-1, keepdims=True))).astype(bf16)
    d_query = (
        (
            jnp.einsum("hqk,khd->qhd", d_scores, split_heads(keys), preferred_element_type=f32)
            * 0.125
        )
        .reshape(length, width)
        .astype(bf16)
    )
    d_keys = (
        (
            jnp.einsum("hqk,qhd->khd", d_scores, split_heads(query), preferred_element_type=f32)
            * 0.125
        )
        .reshape(length, width)
        .astype(bf16)
    )
    d_values = (
        jnp.einsum("hqk,qhd->khd", probs_low, d_attended, preferred_element_type=f32)
        .reshape(length, width)
        .astype(bf16)
    )
    grads["query_bias"] = jnp.sum(d_query.astype(f32), axis=0)
    grads["value_bias"] = jnp.sum(d_values.astype(f32), axis=0)
    input_grad = (
        d_branch_full
        + backdot(d_query, params["query_weight"])
        + backdot(d_keys, params["key_weight"])
        + backdot(d_values, params["value_weight"])
    )
    def by_owner(value):
        return value.astype(bf16).reshape(n, -1, width)

    row = lax.broadcasted_iota(jnp.int32, (n, total_rows - used, width), 1)
    flat = jnp.zeros((n, total_rows - used, width), f32)
    for k, name in enumerate(VECTORS):
        mine = grads[name].reshape(n, -1)
        mine = jnp.pad(mine, ((0, 0), (0, width - mine.shape[1])))
        flat = jnp.where(row == k, mine[:, None, :], flat)
    flat = flat.astype(bf16)
    operands = (tokens, d_query, d_keys, d_values, attended, d_branch, first_low, d_hidden, active, d_down, flat)
    even = part % 8 == 0 and tall % 16 == 0 and wide % 2 == 0
    if even and width % math.lcm(part, 128) == 0 and up_weight.shape[1] % math.lcm(tall, 128) == 0:
        terms = terms_by_owner(part, tall, total_rows, operands)
    else:
        up = rowdot(first_low, d_hidden)
        terms = jnp.concatenate(
            [by_owner(rowdot(tokens, grad)) for grad in (d_query, d_keys, d_values)]
            + [by_owner(rowdot(attended, d_branch))]
            + [by_owner(up[:, j * width : (j + 1) * width]) for j in range(wide)]
            + [by_owner(rowdot(active, d_down)), flat],
            axis=1,
        )
    sums = sum_shards(dp, fsdp, terms)
    owned = {}
    for k, name in enumerate(("query", "key", "value", "out")):
        owned[name + "_weight"] = sums[k * part : (k + 1) * part]
    owned["up_weight"] = jnp.concatenate(
        [sums[(4 + j) * part : (5 + j) * part] for j in range(wide)], axis=1
    )
    owned["down_weight"] = sums[(4 + wide) * part : used]
    for k, name in enumerate(VECTORS):
        owned[name] = sums[used + k, : given[name].shape[0]]
    return tuple([layer_output, input_grad] + [owned[name] for name in PARAM_NAMES])


def solution(mesh):
    in_specs = (
        P(("dp", "fsdp"), None),
        P(("dp", "fsdp"), None),
        P(("dp", "fsdp"), None),
        P(("dp", "fsdp"), None),
        P(("dp", "fsdp")),
        P(("dp", "fsdp")),
        P(("dp", "fsdp"), None),
        P(("dp", "fsdp")),
        P(("dp", "fsdp")),
        P(("dp", "fsdp")),
        P(("dp", "fsdp"), None),
        P(("dp", "fsdp")),
        P(("dp", "fsdp"), None),
        P(("dp", "fsdp")),
        P(("dp", "fsdp")),
        P(("dp", "fsdp")),
        P(("dp", "fsdp"), None),
        P(("dp", "fsdp"), None),
    )
    out_specs = (
        P(("dp", "fsdp"), None),
        P(("dp", "fsdp"), None),
        P(("dp", "fsdp"), None),
        P(("dp", "fsdp"), None),
        P(("dp", "fsdp"), None),
        P(("dp", "fsdp")),
        P(("dp", "fsdp")),
        P(("dp", "fsdp"), None),
        P(("dp", "fsdp")),
        P(("dp", "fsdp")),
        P(("dp", "fsdp")),
        P(("dp", "fsdp"), None),
        P(("dp", "fsdp")),
        P(("dp", "fsdp"), None),
        P(("dp", "fsdp")),
        P(("dp", "fsdp")),
        P(("dp", "fsdp")),
    )
    return jax.shard_map(
        partial(on_device, mesh.shape["dp"], mesh.shape["fsdp"]),
        mesh=mesh,
        in_specs=in_specs,
        out_specs=out_specs,
        check_vma=False,
    )
```
